512 devices in a mesh: section: 32 (over y, z_lo), row: 4 (over z_hi, core), col: 4 (over x).
Axes of the slice: x: 4, y: 4, z: 16 (z_hi: 2, z_lo: 8; z = z_hi * 8 + z_lo), core: 2. Of those that a mesh axis runs over, the one named last changes fastest.
Arguments:
- inputs: bfloat16 [512, 6144], P('row', 'col'), may hold values from -6 to 6
- cotangent: bfloat16 [512, 6144], P('row', 'col'), may hold values from -3 to 3
- ln_gain: float32 [6144], P('col'), may hold values from 0.1 to 1.9
- ln_bias: float32 [6144], P('col'), may hold values from -3 to 3
- w_in: bfloat16 [6144, 24576], P('row', ('section', 'col')), may hold values from -0.078125 to 0.078125
- w_out: bfloat16 [24576, 6144], P(('section', 'row'), 'col'), may hold values from -0.0390625 to 0.0390625
Outputs:
- outputs: bfloat16 [512, 6144], P('row', 'col')
- grad_x: bfloat16 [512, 6144], P('row', 'col')
- grad_in: bfloat16 [6144, 24576], P('row', ('section', 'col'))
- grad_out: bfloat16 [24576, 6144], P(('section', 'row'), 'col')
The draws below stay inside these ranges and needn't reach their ends.
All inputs are finite; a program needn't handle non-finite values.
Results may differ from the reference program's by a relative error of at most 0.0062.
Values may be sent and summed in bfloat16 or wider, within the bound.
A program may use at most 64 MiB of HBM per device.

```python
import jax
import jax.numpy as jnp
from jax import lax

D = 6144
HID = 24576
MBTOK = 512


def block_scale(key, dims, cuts, smallest, high):
    factor_of, own = 1.0, jax.random.fold_in(key, 6)
    for axis_at, shards_of in cuts:
        steps = jnp.exp(jax.random.uniform(jax.random.fold_in(own, axis_at), (shards_of,), jnp.float32, smallest / len(cuts), high / len(cuts)))
        factor_of = factor_of * jnp.repeat(steps, dims[axis_at] // shards_of).reshape([-1 if axis == axis_at else 1 for axis in range(len(dims))])
    return factor_of


def gaussian(stream_key, extent, width, bound, cuts=(), dtype=jnp.bfloat16):
    drawn = width * jax.random.normal(stream_key, extent, jnp.float32)
    if cuts:
        drawn = drawn * block_scale(stream_key, extent, cuts, -0.22, 0.18)
    return jnp.clip(drawn, -bound, bound).astype(dtype)


def setup_inputs(seed: int = 0) -> dict:
    streams_of = jax.random.split(jax.random.key(seed), 7)
    return {
        "inputs": gaussian(streams_of[0], (MBTOK, D), 1.0, 6.0, ((0, 4), (1, 4))),
        "cotangent": gaussian(streams_of[1], (MBTOK, D), 0.2, 3.0, ((0, 4), (1, 4))),
        "ln_gain": jnp.clip(1.0 + 0.18 * jax.random.normal(streams_of[2], (D,), jnp.float32), 0.1, 1.9),
        "ln_bias": gaussian(streams_of[3], (D,), 0.5, 3.0, ((0, 4),), jnp.float32),
        "w_in": gaussian(streams_of[4], (D, HID), D ** -0.5, 0.078125, ((0, 4), (1, 128))),
        "w_out": gaussian(streams_of[5], (HID, D), HID ** -0.5, 0.0390625, ((0, 128), (1, 4))),
    }


EPS = 1e-05
SLOPE = 0.7978845608028654
CUBIC = 0.044715

def gelu(values):
    return 0.5 * values * (1.0 + jnp.tanh(SLOPE * (values + CUBIC * values * values * values)))

def gelu_slope(values):
    inner = jnp.tanh(SLOPE * (values + CUBIC * values * values * values))
    return 0.5 * (1.0 + inner) + 0.5 * values * (1.0 - inner * inner) * SLOPE * (1.0 + 3.0 * CUBIC * values * values)

def reference(inputs, cotangent, ln_gain, ln_bias, w_in, w_out):
    stream_f32 = inputs.astype(jnp.float32)
    row_mean = lax.optimization_barrier(jnp.mean(stream_f32, -1, keepdims=True))
    second = lax.optimization_barrier(jnp.mean(stream_f32 * stream_f32, -1, keepdims=True))
    inv_scale = lax.rsqrt(second - row_mean * row_mean + EPS)
    scaled = (stream_f32 - row_mean) * inv_scale
    normed = (scaled * ln_gain + ln_bias).astype(jnp.bfloat16)
    hidden = jnp.dot(normed, w_in, preferred_element_type=jnp.float32)
    active = gelu(hidden).astype(jnp.bfloat16)
    outputs = (stream_f32 + jnp.dot(active, w_out, preferred_element_type=jnp.float32)).astype(jnp.bfloat16)
    grad_act = jnp.dot(cotangent, w_out.T, preferred_element_type=jnp.float32)
    grad_hid = (grad_act * gelu_slope(hidden)).astype(jnp.bfloat16)
    grad_norm = jnp.dot(grad_hid, w_in.T, preferred_element_type=jnp.float32)
    grad_scaled = grad_norm * ln_gain
    first_mean = lax.optimization_barrier(jnp.mean(grad_scaled, -1, keepdims=True))
    second_mean = lax.optimization_barrier(jnp.mean(grad_scaled * scaled, -1, keepdims=True))
    delta = inv_scale * (grad_scaled - first_mean - scaled * second_mean)
    grad_x = (cotangent.astype(jnp.float32) + delta).astype(jnp.bfloat16)
    grad_in = jnp.dot(normed.T, grad_hid, preferred_element_type=jnp.float32).astype(jnp.bfloat16)
    grad_out = jnp.dot(active.T, cotangent, preferred_element_type=jnp.float32).astype(jnp.bfloat16)
    return (outputs, grad_x, grad_in, grad_out)
```

```python
import functools

import jax
import jax.numpy as jnp
from jax import lax
from jax.experimental import pallas as pl
from jax.experimental.pallas import tpu as pltpu
from jax.sharding import PartitionSpec as P

EPS = 1e-05
SLOPE = 0.7978845608028654
CUBIC = 0.044715
F32, BF16 = jnp.float32, jnp.bfloat16
NX, NY, NZ, NL = 4, 4, 16, 8
TOK, FEAT, HIDT = 128, 1536, 192
D = NX * FEAT
QR = TOK // NY
PR, PC = TOK // NL, FEAT // NY
VMEM = pl.BlockSpec(memory_space=pltpu.VMEM)
NT = (((1,), (1,)), ((), ()))
TN = (((0,), (0,)), ((), ()))


def gelu_both(values):
    inner = jnp.tanh(SLOPE * (values + CUBIC * values * values * values))
    act = 0.5 * values * (1.0 + inner)
    slope = 0.5 * (1.0 + inner) + 0.5 * values * (1.0 - inner * inner) * SLOPE * (
        1.0 + 3.0 * CUBIC * values * values
    )
    return act, slope


def place():
    section, row, x = lax.axis_index("section"), lax.axis_index("row"), lax.axis_index("col")
    y, zl = lax.div(section, NL), lax.rem(section, NL)
    zh, k = lax.div(row, 2), lax.rem(row, 2)
    return x, y, zh * NL + zl, zh, zl, k, row


def dev(x, y, z, k):
    return (y * NL + lax.rem(z, NL), lax.div(z, NL) * 2 + k, x)


def send(src, dst, ssem, rsem, to):
    copy = pltpu.make_async_remote_copy(
        src_ref=src, dst_ref=dst, send_sem=ssem, recv_sem=rsem,
        device_id=to, device_id_type=pl.DeviceIdType.MESH,
    )
    copy.start()
    return copy


def arrived(ref, sem):
    pltpu.make_async_copy(ref, ref, sem).wait()


def meet(peers, turned=None, diag=None):
    barrier = pltpu.get_barrier_semaphore()

    def greet(some):
        for peer in some:
            pl.semaphore_signal(barrier, inc=1, device_id=peer, device_id_type=pl.DeviceIdType.MESH)
        pl.semaphore_wait(barrier, len(some))

    if turned is None:
        greet(peers)
    else:
        pl.when(diag)(lambda: greet(peers))
        pl.when(jnp.logical_not(diag))(lambda: greet(peers + [turned]))


def al(value, mult):
    return pl.multiple_of(value, mult)


def pack_pair(first, second):
    lane = lax.broadcasted_iota(jnp.int32, (TOK, TOK), 1)
    both = jnp.where(lane == 0, first, jnp.where(lane == 1, second, 0.0))
    return both.T[0:8, :]


def unpack_pair(packed):
    both = jnp.concatenate([packed, jnp.zeros((TOK - 8, TOK), F32)], axis=0).T
    return both[:, 0:1], both[:, 1:2]


def share_kernel(x_ref, cot_ref, gain_ref, bias_ref, X, C, st_ref, xn, sums, ssem, rsem):
    x, y, z, zh, zl, k, r = place()
    zm = NZ - 1 - z
    xs = [lax.rem(x + d, NX) for d in (1, 2, 3)]
    ys = [lax.rem(y + d, NY) for d in (1, 2, 3)]
    meet(
        [dev(p, y, z, k) for p in xs]
        + [dev(x, p, z, k) for p in ys]
        + [dev(x, y, z, 1 - k), dev(x, y, zm, k), dev(x, y, zm, 1 - k)]
    )
    q = pl.ds(al(y * QR, QR), QR)
    sent = []
    tile_of = [zh * 2 + k, zh * 2 + 1 - k, (1 - zh) * 2 + k, (1 - zh) * 2 + 1 - k]
    sent.append(send(cot_ref.at[q], C.at[r, q], ssem.at[0], rsem.at[0], dev(x, y, zm, k)))
    sent.append(send(cot_ref, C.at[r], ssem.at[1], rsem.at[1], dev(x, y, z, 1 - k)))
    rows = x_ref[...].astype(F32)
    sums[0] = pack_pair(
        jnp.sum(rows, -1, keepdims=True), jnp.sum(rows * rows, -1, keepdims=True)
    )
    for i, p in enumerate(xs):
        sent.append(send(sums.at[0], sums.at[1 + i], ssem.at[2 + i], rsem.at[2 + i], dev(p, y, z, k)))
    C[r] = cot_ref[...]
    for i in range(3):
        arrived(sums.at[1 + i], rsem.at[2 + i])
    first, second = unpack_pair((sums[0] + sums[1]) + (sums[2] + sums[3]))
    mean = first / D
    rstd = lax.rsqrt(second / D - mean * mean + EPS)
    lane = lax.broadcasted_iota(jnp.int32, (TOK, TOK), 1)
    st_ref[...] = jnp.where(lane == 0, mean, rstd)
    xn[...] = ((x_ref[...].astype(F32) - mean) * rstd * gain_ref[...] + bias_ref[...]).astype(BF16)
    diag = r == x
    zb, kb = lax.div(x, 2), lax.rem(x, 2)
    across = (zb != zh).astype(jnp.int32)
    delta = across * 2 + (kb != k).astype(jnp.int32)
    ztarget = zb * NL + jnp.where(zb == zh, zl, NL - 1 - zl)
    XQ, YQ, YC = 5, 9, 21

    @pl.when(jnp.logical_not(diag))
    def _():
        send(xn.at[q], X.at[r, q], ssem.at[5], rsem.at[XQ + delta], dev(x, y, ztarget, kb))

    @pl.when(diag)
    def _():
        X[r, q, :] = xn[q, :]

    def cot_out():
        arrived(C.at[tile_of[2], q], rsem.at[0])
        for i, p in enumerate(ys):
            part = C.at[tile_of[2], q]
            sent.append(send(part, part, ssem.at[30 + i], rsem.at[YC + i], dev(x, p, z, k)))

    for d in range(4):
        part = X.at[tile_of[d], q]
        if d == 0:
            @pl.when(jnp.logical_not(diag))
            def _():
                arrived(part, rsem.at[XQ])
        else:
            arrived(part, rsem.at[XQ + d])

        @pl.when(diag)
        def _():
            for i, p in enumerate(xs):
                send(part, part, ssem.at[6 + d * 3 + i], rsem.at[XQ + d], dev(p, y, z, k))

        for i, p in enumerate(ys):
            sent.append(
                send(part, part, ssem.at[18 + d * 3 + i], rsem.at[YQ + d * 3 + i], dev(x, p, z, k))
            )
        if d == 1:
            cot_out()
    for i in range(3):
        src_y = lax.rem(y + NY - 1 - i, NY)
        arrived(C.at[tile_of[2], pl.ds(al(src_y * QR, QR), QR)], rsem.at[YC + i])
    sent.append(send(C.at[tile_of[2]], C.at[tile_of[2]], ssem.at[33], rsem.at[24], dev(x, y, z, 1 - k)))
    for d in range(4):
        for i in range(3):
            src_y = lax.rem(y + NY - 1 - i, NY)
            arrived(X.at[tile_of[d], pl.ds(al(src_y * QR, QR), QR)], rsem.at[YQ + d * 3 + i])
    arrived(C.at[tile_of[1]], rsem.at[1])
    arrived(C.at[tile_of[3]], rsem.at[24])
    for copy in sent:
        copy.wait_send()

    @pl.when(diag)
    def _():
        for d in range(4):
            for i in range(3):
                arrived(X.at[tile_of[d], q], ssem.at[6 + d * 3 + i])

    @pl.when(jnp.logical_not(diag))
    def _():
        arrived(xn.at[q], ssem.at[5])


def hidden_kernel(X, C, w_in, w_out, aT, gT, hs, hr, us, ur, gs, gr, ts, tr, av, ssem, rsem):
    x, y, z, zh, zl, k, r = place()
    zp = (1 - zh) * NL + zl
    xs = [lax.rem(x + d, NX) for d in (1, 2, 3)]
    diag = r == x
    core, pair = dev(x, y, z, 1 - k), dev(x, y, zp, k)
    turned = (lax.axis_index("section"), x, r)
    meet([dev(p, y, z, k) for p in xs] + [core, pair], turned, diag)
    sent = []

    def hid(t):
        return lax.dot_general(w_in[...], X[t], NT, preferred_element_type=F32)

    def grad(t):
        return lax.dot_general(w_out[...], C[t], NT, preferred_element_type=F32)

    for i, t in enumerate(((1 - zh) * 2 + 1 - k, zh * 2 + 1 - k)):
        hs[i] = hid(t)
        sent.append(send(hs.at[i], hr.at[i], ssem.at[i], rsem.at[i], core))
    for i in (1, 0, 2):
        gs[i] = grad(xs[i]).astype(BF16)
        sent.append(send(gs.at[i], gr.at[i], ssem.at[2 + i], rsem.at[2 + i], dev(xs[i], y, z, k)))
    far = hid((1 - zh) * 2 + k)
    arrived(hr.at[0], rsem.at[0])
    us[...] = (far + hr[0]).astype(BF16)
    sent.append(send(us, ur, ssem.at[5], rsem.at[5], pair))
    own_grad = grad(x)
    for i in range(3):
        arrived(gr.at[i], rsem.at[2 + i])
    own_grad = own_grad + gr[0].astype(F32) + gr[1].astype(F32) + gr[2].astype(F32)
    ts[...] = own_grad.astype(BF16)

    @pl.when(diag)
    def _():
        tr[...] = ts[...]

    @pl.when(jnp.logical_not(diag))
    def _():
        send(ts, tr, ssem.at[6], rsem.at[6], turned)

    near = hid(r)
    arrived(hr.at[1], rsem.at[1])
    near = near + hr[1]
    arrived(ur, rsem.at[5])
    act, slope = gelu_both(near + ur[...].astype(F32))
    av[...] = act.astype(BF16)

    @pl.when(diag)
    def _():
        aT[r] = av[...]

    @pl.when(jnp.logical_not(diag))
    def _():
        send(av, aT.at[r], ssem.at[7], rsem.at[7], turned)
        arrived(tr, rsem.at[6])

    gT[r] = (tr[...].astype(F32) * slope).astype(BF16)
    sent.append(send(gT.at[r], gT.at[r], ssem.at[8], rsem.at[8], pair))
    sent.append(send(gT.at[r], gT.at[r], ssem.at[9], rsem.at[9], core))

    @pl.when(jnp.logical_not(diag))
    def _():
        arrived(aT.at[x], rsem.at[7])

    for i, p in enumerate(xs):
        sent.append(send(aT.at[x], aT.at[x], ssem.at[10 + i], rsem.at[10 + i], dev(p, y, z, k)))
    other = (1 - zh) * 2 + k
    arrived(gT.at[other], rsem.at[8])
    sent.append(send(gT.at[other], gT.at[other], ssem.at[13], rsem.at[13], core))
    arrived(gT.at[zh * 2 + 1 - k], rsem.at[9])
    for i in range(3):
        arrived(aT.at[lax.rem(x + NX - 1 - i, NX)], rsem.at[10 + i])
    arrived(gT.at[(1 - zh) * 2 + 1 - k], rsem.at[13])
    for copy in sent:
        copy.wait_send()

    @pl.when(jnp.logical_not(diag))
    def _():
        arrived(ts, ssem.at[6])
        arrived(av, ssem.at[7])


def total_kernel(
    aT, gT, w_in, w_out, X, C, x_ref, cot_ref, st_ref, gain_ref,
    out, gx, g_in, g_out,
    gs, gr, g0, g1, g1r, g2, g2r, gp, gn,
    os, orr, o0, o1, o1r, o2, o2r, sums,
    ssem, rsem,
):
    x, y, z, zh, zl, k, r = place()
    xs = [lax.rem(x + d, NX) for d in (1, 2, 3)]
    ys = [lax.rem(y + d, NY) for d in (1, 2, 3)]
    zs = [lax.rem(z + d, NZ) for d in range(1, NZ)]
    ls = [lax.rem(zl + d, NL) for d in range(1, NL)]
    diag = r == x
    core = dev(x, y, z, 1 - k)
    turned = (lax.axis_index("section"), x, r)
    meet(
        [dev(p, y, z, k) for p in xs] + [dev(x, p, z, k) for p in ys]
        + [dev(x, y, p, k) for p in zs] + [core],
        turned, diag,
    )
    sent = []
    count = [0]

    def put(src, dst, rslot, to):
        sent.append(send(src, dst, ssem.at[count[0]], rsem.at[rslot], to))
        count[0] += 1

    GX, OC, OY, GY, OZ, GL, GT = 0, 3, 5, 8, 11, 26, 33
    OAL, OAY, GAL, GAY, ST = 34, 41, 44, 51, 54

    def part_g(t):
        return lax.dot_general(gT[t], w_in[...], TN, preferred_element_type=F32)

    def part_o(t):
        return lax.dot_general(aT[t], w_out[...], TN, preferred_element_type=F32)

    def cols(p):
        return pl.ds(al(p * PC, PC), PC)

    def prow(p):
        return pl.ds(al(p * PR, PR), PR)

    for i in (1, 0, 2):
        gs[i] = part_g(xs[i]).astype(BF16)
        put(gs.at[i], gr.at[i], GX + i, dev(xs[i], y, z, k))
    for i in range(2):
        os[i] = part_o(i * 2 + 1 - k).astype(BF16)
        put(os.at[i], orr.at[i], OC + i, core)
    for i in range(2):
        o0[i] = part_o(i * 2 + k)
    for i in range(2):
        arrived(orr.at[i], rsem.at[OC + i])
    o1[...] = (o0[...] + orr[...].astype(F32)).astype(BF16)
    for i, p in enumerate(ys):
        put(o1.at[:, :, cols(p)], o1r.at[i], OY + i, dev(x, p, z, k))
    g0[...] = part_g(x)
    acc = jnp.zeros((HIDT, FEAT), F32)
    for t in range(4):
        acc = acc + jnp.dot(aT[t], C[t], preferred_element_type=F32)
    g_out[...] = acc.astype(BF16)
    for i in range(3):
        arrived(o1r.at[i], rsem.at[OY + i])
    o2[...] = (
        o1[:, :, cols(y)].astype(F32) + o1r[0].astype(F32) + o1r[1].astype(F32) + o1r[2].astype(F32)
    ).astype(BF16)
    for i, p in enumerate(zs):
        put(o2.at[lax.div(p, NL), prow(lax.rem(p, NL))], o2r.at[i], OZ + i, dev(x, y, p, k))
    acc = jnp.zeros((HIDT, FEAT), F32)
    for t in range(4):
        acc = acc + jnp.dot(gT[t], X[t], preferred_element_type=F32)
    g_in[...] = acc.astype(BF16)
    for i in range(3):
        arrived(gr.at[i], rsem.at[GX + i])
    g1[...] = (g0[...] + gr[0].astype(F32) + gr[1].astype(F32) + gr[2].astype(F32)).astype(BF16)
    for i, p in enumerate(ys):
        put(g1.at[:, cols(p)], g1r.at[i], GY + i, dev(x, p, z, k))
    for i in range(NZ - 1):
        arrived(o2r.at[i], rsem.at[OZ + i])
    piece = o2[zh, prow(zl), :].astype(F32)
    for i in range(NZ - 1):
        piece = piece + o2r[i].astype(F32)
    mine = (prow(zl), cols(y))
    out[mine] = (x_ref[mine].astype(F32) + piece).astype(BF16)
    for i, p in enumerate(ls):
        put(out.at[mine], out.at[mine], OAL + i, dev(x, y, zh * NL + p, k))
    for i in range(3):
        arrived(g1r.at[i], rsem.at[GY + i])
    g2[...] = (
        g1[:, cols(y)].astype(F32) + g1r[0].astype(F32) + g1r[1].astype(F32) + g1r[2].astype(F32)
    ).astype(BF16)
    for i, p in enumerate(ls):
        put(g2.at[prow(p)], g2r.at[i], GL + i, dev(x, y, zh * NL + p, k))
    for i in range(NL - 1):
        arrived(g2r.at[i], rsem.at[GL + i])
    piece = g2[prow(zl), :].astype(F32)
    for i in range(NL - 1):
        piece = piece + g2r[i].astype(F32)
    gp[...] = piece.astype(BF16)

    @pl.when(diag)
    def _():
        gn[mine] = gp[...]

    @pl.when(jnp.logical_not(diag))
    def _():
        send(gp, gn.at[mine], ssem.at[63], rsem.at[GT], turned)

    for i in range(NL - 1):
        src = lax.rem(zl + NL - 1 - i, NL)
        arrived(out.at[prow(src), cols(y)], rsem.at[OAL + i])
    for i, p in enumerate(ys):
        put(out.at[:, cols(y)], out.at[:, cols(y)], OAY + i, dev(x, p, z, k))

    @pl.when(jnp.logical_not(diag))
    def _():
        arrived(gn.at[mine], rsem.at[GT])

    for i, p in enumerate(ls):
        put(gn.at[mine], gn.at[mine], GAL + i, dev(x, y, zh * NL + p, k))
    for i in range(NL - 1):
        src = lax.rem(zl + NL - 1 - i, NL)
        arrived(gn.at[prow(src), cols(y)], rsem.at[GAL + i])
    for i, p in enumerate(ys):
        put(gn.at[:, cols(y)], gn.at[:, cols(y)], GAY + i, dev(x, p, z, k))
    mean, rstd = st_ref[:, 0:1], st_ref[:, 1:2]
    scaled = (x_ref[...].astype(F32) - mean) * rstd
    for i in range(3):
        src = lax.rem(y + NY - 1 - i, NY)
        arrived(gn.at[:, cols(src)], rsem.at[GAY + i])
    gz = gn[...].astype(F32) * gain_ref[...]
    sums[0] = pack_pair(
        jnp.sum(gz, -1, keepdims=True), jnp.sum(gz * scaled, -1, keepdims=True)
    )
    for i, p in enumerate(xs):
        put(sums.at[0], sums.at[1 + i], ST + i, dev(p, y, z, k))
    for i in range(3):
        src = lax.rem(y + NY - 1 - i, NY)
        arrived(out.at[:, cols(src)], rsem.at[OAY + i])
    for i in range(3):
        arrived(sums.at[1 + i], rsem.at[ST + i])
    first, second = unpack_pair((sums[0] + sums[1]) + (sums[2] + sums[3]))
    delta = rstd * (gz - first / D - scaled * (second / D))
    gx[...] = (cot_ref[...].astype(F32) + delta).astype(BF16)
    for copy in sent:
        copy.wait_send()

    @pl.when(jnp.logical_not(diag))
    def _():
        arrived(gp, ssem.at[63])


def per_device(inputs, cotangent, ln_gain, ln_bias, w_in, w_out):
    gain, bias = ln_gain.reshape(1, FEAT), ln_bias.reshape(1, FEAT)
    w_in_t = w_in.T
    dma = pltpu.SemaphoreType.DMA

    def params(number):
        return pltpu.CompilerParams(
            collective_id=number, has_side_effects=True, vmem_limit_bytes=48 << 20
        )

    wide = jax.ShapeDtypeStruct((4, TOK, FEAT), BF16)
    X, C, stats = pl.pallas_call(
        share_kernel,
        name="share",
        out_shape=[wide, wide, jax.ShapeDtypeStruct((TOK, TOK), F32)],
        in_specs=[VMEM] * 4,
        out_specs=[VMEM] * 3,
        scratch_shapes=[
            pltpu.VMEM((TOK, FEAT), BF16),
            pltpu.VMEM((4, 8, TOK), F32),
            dma((34,)),
            dma((25,)),
        ],
        compiler_params=params(0),
    )(inputs, cotangent, gain, bias)
    small = jax.ShapeDtypeStruct((4, HIDT, TOK), BF16)
    one = pltpu.VMEM((HIDT, TOK), BF16)
    aT, gT = pl.pallas_call(
        hidden_kernel,
        name="hidden",
        out_shape=[small, small],
        in_specs=[VMEM] * 4,
        out_specs=[VMEM] * 2,
        scratch_shapes=[
            pltpu.VMEM((2, HIDT, TOK), F32),
            pltpu.VMEM((2, HIDT, TOK), F32),
            one, one,
            pltpu.VMEM((3, HIDT, TOK), BF16),
            pltpu.VMEM((3, HIDT, TOK), BF16),
            one, one, one,
            dma((14,)),
            dma((14,)),
        ],
        compiler_params=params(1),
    )(X, C, w_in_t, w_out)
    tile = jax.ShapeDtypeStruct((TOK, FEAT), BF16)
    grad = jax.ShapeDtypeStruct((HIDT, FEAT), BF16)

    def vb(*shape):
        return pltpu.VMEM(shape, BF16)

    out, gx, g_in, g_out = pl.pallas_call(
        total_kernel,
        name="total",
        out_shape=[tile, tile, grad, grad],
        in_specs=[VMEM] * 10,
        out_specs=[VMEM] * 4,
        scratch_shapes=[
            vb(3, TOK, FEAT), vb(3, TOK, FEAT), pltpu.VMEM((TOK, FEAT), F32),
            vb(TOK, FEAT), vb(3, TOK, PC), vb(TOK, PC), vb(NL - 1, PR, PC), vb(PR, PC), vb(TOK, FEAT),
            vb(2, TOK, FEAT), vb(2, TOK, FEAT), pltpu.VMEM((2, TOK, FEAT), F32),
            vb(2, TOK, FEAT), vb(3, 2, TOK, PC), vb(2, TOK, PC), vb(NZ - 1, PR, PC),
            pltpu.VMEM((4, 8, TOK), F32),
            dma((64,)),
            dma((57,)),
        ],
        compiler_params=params(2),
    )(aT, gT, w_in_t, w_out, X, C, inputs, cotangent, stats, gain)
    return out, gx, g_in.T, g_out


def solution(mesh):
    return jax.shard_map(
        per_device,
        mesh=mesh,
        in_specs=(
            P("row", "col"),
            P("row", "col"),
            P("col"),
            P("col"),
            P("row", ("section", "col")),
            P(("section", "row"), "col"),
        ),
        out_specs=(
            P("row", "col"),
            P("row", "col"),
            P("row", ("section", "col")),
            P(("section", "row"), "col"),
        ),
        check_vma=False,
    )
```

```python
import jax
import jax.numpy as jnp
from jax import lax
from jax.experimental import pallas as pl
from jax.experimental.pallas import tpu as pltpu
from jax.sharding import PartitionSpec as P

EPS = 1e-05
SLOPE = 0.7978845608028654
CUBIC = 0.044715
F32, BF16 = jnp.float32, jnp.bfloat16
NX, NY, NZ, NL = 4, 4, 16, 8
TOK, FEAT, HIDT = 128, 1536, 192
D = NX * FEAT
QR = TOK // NY
PR, PC = TOK // NL, FEAT // NY
ANY = pl.BlockSpec(memory_space=pl.ANY)
NT = (((1,), (1,)), ((), ()))


def gelu_both(values):
    inner = jnp.tanh(SLOPE * (values + CUBIC * values * values * values))
    act = 0.5 * values * (1.0 + inner)
    slope = 0.5 * (1.0 + inner) + 0.5 * values * (1.0 - inner * inner) * SLOPE * (
        1.0 + 3.0 * CUBIC * values * values
    )
    return act, slope


def place():
    section, row, x = lax.axis_index("section"), lax.axis_index("row"), lax.axis_index("col")
    y, zl = lax.div(section, NL), lax.rem(section, NL)
    zh, k = lax.div(row, 2), lax.rem(row, 2)
    return x, y, zh * NL + zl, zh, zl, k, row


def dev(x, y, z, k):
    return (y * NL + lax.rem(z, NL), lax.div(z, NL) * 2 + k, x)

def al(value, mult):
    return pl.multiple_of(value, mult)


def pack_pair(first, second):
    lane = lax.broadcasted_iota(jnp.int32, (TOK, TOK), 1)
    both = jnp.where(lane == 0, first, jnp.where(lane == 1, second, 0.0))
    return both.T[0:8, :]


def unpack_pair(packed):
    both = jnp.concatenate([packed, jnp.zeros((TOK - 8, TOK), F32)], axis=0).T
    return both[:, 0:1], both[:, 1:2]


def arrived(ref, sem):
    pltpu.make_async_copy(ref, ref, sem).wait()


class Wires:
    def __init__(self, ssem, rsem):
        self.ssem, self.rsem = ssem, rsem
        self.slots, self.sent = {}, []

    def slot(self, *name):
        return self.rsem.at[self.slots.setdefault(name, len(self.slots))]

    def put(self, make, name, pred=None):
        rsem, ssem = self.slot(*name), self.ssem.at[len(self.sent)]

        src, dst, to = make()

        def copy():
            return pltpu.make_async_remote_copy(
                src_ref=src, dst_ref=dst, send_sem=ssem, recv_sem=rsem,
                device_id=to, device_id_type=pl.DeviceIdType.MESH,
            )

        when(pred, lambda: copy().start())
        self.sent.append((pred, copy))

    def got(self, make, name, pred=None):
        ref, sem = make(), self.slot(*name)
        when(pred, lambda: arrived(ref, sem))

    def finish(self):
        for pred, copy in self.sent:
            when(pred, lambda copy=copy: copy().wait_send())


def when(pred, act):
    if pred is None:
        act()
    else:
        pl.when(pred)(act)


def tpos(t):
    return lax.rem(t, 2) * 2 + lax.div(t, 2)


N_SEND, N_RECV = 190, 160


def layer_kernel(
    x_any, cot_any, gain_any, bias_any, win_any, wout_any,
    out_any, gx_any, gin_any, gout_any,
    x_ref, cot_ref, gain_ref, bias_ref, w_in, w_out,
    X, C, xn, sums, st_ref,
    hs, hr, us, ur, qs, qr, ts, tr, gT, aT, gt, at,
    gs, gr, g0, g1, g1r, g2, g2r, gp, gn,
    os, orr, o0, o1, o1r, o2, o2r, stats, out, gx, g_in, g_out,
    ssem, rsem, lsem,
):
    x, y, z, zh, zl, k, r = place()
    no = jnp.logical_not
    w = Wires(ssem, rsem)
    put, got = w.put, w.got
    loads = [
        pltpu.make_async_copy(src, dst, lsem.at[i])
        for i, (src, dst) in enumerate((
            (x_any, x_ref), (cot_any, cot_ref), (gain_any, gain_ref),
            (bias_any, bias_ref), (win_any, w_in), (wout_any, w_out),
        ))
    ]
    for load in loads:
        load.start()
    zm, zp = NZ - 1 - z, (1 - zh) * NL + zl
    par = lax.rem(zl, 2)
    zn = z + 1 - 2 * par
    xs = [lax.rem(x + d, NX) for d in (1, 2, 3)]
    ys = [lax.rem(y + d, NY) for d in (1, 2, 3)]
    zs = [lax.rem(z + d, NZ) for d in range(1, NZ)]
    ls = [lax.rem(zl + d, NL) for d in range(NL)]
    diag = r == x
    zb, kb = lax.div(x, 2), lax.rem(x, 2)
    home = zb == zh
    beside = jnp.logical_and(home, k != kb)
    core, pair = dev(x, y, z, 1 - k), dev(x, y, zp, k)

    barrier = pltpu.get_barrier_semaphore()

    def greet(peer, pred=None):
        when(pred, lambda: pl.semaphore_signal(
            barrier, inc=1, device_id=peer, device_id_type=pl.DeviceIdType.MESH))

    for p in zs:
        greet(dev(x, y, p, k))
    greet(core)
    greet(dev(x, y, zm, 1 - k))
    for dx in range(4):
        for dy in range(4):
            if dx or dy:
                greet(dev(lax.rem(x + dx, NX), lax.rem(y + dy, NY), z, k))
    section = lax.axis_index("section")
    for half in range(2):
        greet((section, x, half * 2 + k), no(jnp.logical_and(diag, zh == half)))
    greet(dev(r, y, z, 1 - k), no(diag))
    for d in range(NL):
        greet(dev(r, y, zh * NL + ls[d], kb), no(diag) if d == 0 else None)
    def num(flag):
        return flag.astype(jnp.int32)
    total = 15 + 2 + 15 + 2 - num(diag) + 3 * num(beside) + 16 * num(home) - num(diag)

    loads[0].wait()
    rows = x_ref[...].astype(F32)
    sums[0] = pack_pair(
        jnp.sum(rows, -1, keepdims=True), jnp.sum(rows * rows, -1, keepdims=True)
    )
    loads[1].wait()
    loads[2].wait()
    loads[3].wait()
    pl.semaphore_wait(barrier, total)

    def rows_at(start, size):
        return pl.ds(al(start, 16), size)

    mine8 = rows_at(y * QR + par * 16, 16)
    theirs8 = rows_at(y * QR + (1 - par) * 16, 16)
    quarter = rows_at(y * QR, QR)
    front, back = pl.ds(0, 64), rows_at(64 + y * 16, 16)
    tiles = [zh * 2 + k, zh * 2 + 1 - k, (1 - zh) * 2 + k, (1 - zh) * 2 + 1 - k]

    for i, p in enumerate(xs):
        put(lambda: (sums.at[0], sums.at[1 + i], dev(p, y, z, k)), ("stat", i))
    put(lambda: (cot_ref.at[mine8], C.at[r, mine8], dev(x, y, zm, k)), ("cz",))
    put(lambda: (cot_ref, C.at[r], core), ("cc",))
    C[r] = cot_ref[...]
    for i in range(3):
        got(lambda: sums.at[1 + i], ("stat", i))
    first, second = unpack_pair((sums[0] + sums[1]) + (sums[2] + sums[3]))
    mean = first / D
    rstd = lax.rsqrt(second / D - mean * mean + EPS)
    lane = lax.broadcasted_iota(jnp.int32, (TOK, TOK), 1)
    st_ref[...] = jnp.where(lane == 0, mean, rstd)
    gain = gain_ref[...].reshape(1, FEAT)
    bias = bias_ref[...].reshape(1, FEAT)
    xn[...] = ((x_ref[...].astype(F32) - mean) * rstd * gain + bias).astype(BF16)

    away = no(home)
    for j in range(2):
        put(lambda: (xn.at[mine8], X.at[r, mine8], dev(x, y, zm, k if j == 0 else 1 - k)),
            ("xz", j), jnp.logical_and(away, (k == kb) if j == 0 else (k != kb)))
    put(lambda: (xn.at[back], X.at[r, back], core), ("xb", 1), beside)
    put(lambda: (xn.at[front], X.at[r, front], core), ("xf", 1), beside)

    @pl.when(diag)
    def _():
        X[r, back, :] = xn[back, :]
        X[r, front, :] = xn[front, :]

    def spread(ref, name):
        for i, p in enumerate(xs):
            put(lambda: (ref, ref, dev(p, y, z, k)), name, diag)

    def along_y(ref, name):
        for i, p in enumerate(ys):
            put(lambda: (ref, ref, dev(x, p, z, k)), name + (i,))

    for d in range(2):
        ref = X.at[tiles[d], back]
        got(lambda: ref, ("xb", d), no(diag) if d == 0 else None)
        spread(ref, ("xb", d))
        along_y(ref, ("yb", d))
    spread(X.at[tiles[0], front], ("xf", 0))
    got(lambda: X.at[tiles[1], front], ("xf", 1), diag)
    spread(X.at[tiles[1], front], ("xf", 1))
    got(lambda: C.at[tiles[2], theirs8], ("cz",))
    put(lambda: (C.at[tiles[2], theirs8], C.at[tiles[2], theirs8], dev(x, y, zn, k)), ("cn",))
    for d in (2, 3):
        ref = X.at[tiles[d], theirs8]
        got(lambda: ref, ("xz", d - 2), diag)
        put(lambda: (ref, ref, dev(x, y, zn, k)), ("xn", d), diag)
    got(lambda: C.at[tiles[2], mine8], ("cn",))
    along_y(C.at[tiles[2], quarter], ("cy",))
    for d in (2, 3):
        got(lambda: X.at[tiles[d], mine8], ("xn", d), diag)
        spread(X.at[tiles[d], quarter], ("xq", d))
    for d in (2, 3):
        ref = X.at[tiles[d], quarter]
        got(lambda: ref, ("xq", d), no(diag))
        along_y(ref, ("yq", d))
    from_y = [lax.rem(y + NY - 1 - i, NY) for i in range(3)]
    from_x = [lax.rem(x + NX - 1 - i, NX) for i in range(3)]

    loads[4].wait()
    loads[5].wait()
    for d in range(2):
        got(lambda: X.at[tiles[d], front], ("xf", d), no(diag))
        for i in range(3):
            got(lambda: X.at[tiles[d], rows_at(64 + from_y[i] * 16, 16)], ("yb", d, i))

    def hid(t):
        return lax.dot_general(w_in[...], X[t], NT, preferred_element_type=F32)

    def grad(t):
        return lax.dot_general(w_out[...], C[t], NT, preferred_element_type=F32)

    hs[0] = hid(tiles[1])
    put(lambda: (hs.at[0], hr.at[0], core), ("hc", 0))
    near = hid(tiles[0])
    for i in range(3):
        got(lambda: C.at[tiles[2], rows_at(from_y[i] * QR, QR)], ("cy", i))
    put(lambda: (C.at[tiles[2]], C.at[tiles[2]], core), ("cf",))
    got(lambda: hr.at[0], ("hc", 0))
    h_near = near + hr[0]
    us[0] = h_near.astype(BF16)
    put(lambda: (us.at[0], ur.at[1], pair), ("hz", 0))
    hs[2] = h_near
    got(lambda: C.at[tiles[1]], ("cc",))
    got(lambda: C.at[tiles[3]], ("cf",))
    for i in (1, 0, 2):
        qs[i] = grad(xs[i]).astype(BF16)
        put(lambda: (qs.at[i], qr.at[i], dev(xs[i], y, z, k)), ("ga", i))
    own = grad(x)
    for i in range(3):
        got(lambda: qr.at[i], ("ga", i))
    ts[...] = (own + qr[0].astype(F32) + qr[1].astype(F32) + qr[2].astype(F32)).astype(BF16)
    for half in range(2):
        selfish = jnp.logical_and(diag, zh == half)
        for side in range(2):
            put(lambda: (ts, tr.at[side], (section, half * 2 + kb, r)), ("gt", side),
                jnp.logical_and(no(selfish), zb == side))

    @pl.when(diag)
    def _():
        tr[zh] = ts[...]

    for d in (2, 3):
        for i in range(3):
            got(lambda: X.at[tiles[d], rows_at(from_y[i] * QR, QR)], ("yq", d, i))
    hs[1] = hid(tiles[3])
    put(lambda: (hs.at[1], hr.at[1], core), ("hc", 1))
    far = hid(tiles[2])
    got(lambda: hr.at[1], ("hc", 1))
    h_far = far + hr[1]
    us[1] = h_far.astype(BF16)
    put(lambda: (us.at[1], ur.at[0], pair), ("hz", 1))
    hs[3] = h_far
    for side in range(2):
        got(lambda: tr.at[side], ("gt", side), no(jnp.logical_and(diag, zh == side)))

    def activate(step, half):
        act, slope = gelu_both(hs[2 + step] + ur[step].astype(F32))
        gT[k * 2 + half] = (tr[half].astype(F32) * slope).astype(BF16)
        at[half] = act.astype(BF16)

    got(lambda: ur.at[1], ("hz", 0))
    activate(1, 1 - zh)
    put(lambda: (gT.at[k * 2 + 1 - zh], gT.at[k * 2 + 1 - zh], core), ("gc", 1))
    got(lambda: ur.at[0], ("hz", 1))
    activate(0, zh)
    put(lambda: (gT.at[k * 2 + zh], gT.at[k * 2 + zh], core), ("gc", 0))
    held = pl.ds(k * 2, 2)
    for i, p in enumerate(xs):
        put(lambda: (at, aT.at[held], dev(p, y, z, k)), ("ax", 0), diag)
    for i, p in enumerate(xs):
        put(lambda: (at, aT.at[held], dev(p, y, z, 1 - k)), ("ax", 1), beside)
    put(lambda: (at, aT.at[held], core), ("ax", 1), beside)

    @pl.when(diag)
    def _():
        aT[held] = at[...]

    def cols(p):
        return pl.ds(al(p * PC, PC), PC)

    def prow(p):
        return pl.ds(al(p * PR, PR), PR)

    got(lambda: gT.at[(1 - k) * 2 + 1 - zh], ("gc", 1))
    got(lambda: gT.at[(1 - k) * 2 + zh], ("gc", 0))

    for p in range(4):
        gt[p] = gT[p].T
    order = (2, 1, 3, 0)
    for j in order:
        c = cols(lax.rem(y + j, NY))
        for i in (1, 0, 2):
            gs[i, :, c] = jnp.dot(
                gt[tpos(xs[i])], w_in[:, c], preferred_element_type=F32).astype(BF16)
            put(lambda: (gs.at[i, :, c], gr.at[i, :, c], dev(xs[i], y, z, k)), ("gx", j, i))
    g0[...] = jnp.dot(gt[tpos(x)], w_in[...], preferred_element_type=F32)

    got(lambda: aT.at[held], ("ax", 0), no(diag))
    got(lambda: aT.at[pl.ds((1 - k) * 2, 2)], ("ax", 1))
    for p in range(4):
        gt[p] = aT[p].T
    for i in range(2):
        os[i] = jnp.dot(
            gt[(1 - k) * 2 + i], w_out[...], preferred_element_type=F32).astype(BF16)
        put(lambda: (os.at[i], orr.at[i], core), ("oc", i))
    for i in range(2):
        o0[i] = jnp.dot(gt[k * 2 + i], w_out[...], preferred_element_type=F32)
    for i in range(2):
        got(lambda: orr.at[i], ("oc", i))
    o1[...] = (o0[...] + orr[...].astype(F32)).astype(BF16)
    for i, p in enumerate(ys):
        put(lambda: (o1.at[:, :, cols(p)], o1r.at[i], dev(x, p, z, k)), ("oy", i))

    acc = jnp.zeros((HIDT, FEAT), F32)
    for t in range(4):
        acc = acc + jnp.dot(aT[(t % 2) * 2 + t // 2], C[t], preferred_element_type=F32)
    g_out[...] = acc.astype(BF16)
    stores = [pltpu.make_async_copy(g_out, gout_any, lsem.at[6])]
    stores[0].start()

    def sum_x(j):
        c = cols(lax.rem(y + j, NY))
        for i in range(3):
            got(lambda: gr.at[i, :, c], ("gx", j, i))
        g1[:, c] = (
            g0[:, c] + gr[0, :, c].astype(F32) + gr[1, :, c].astype(F32) + gr[2, :, c].astype(F32)
        ).astype(BF16)
        if j:
            put(lambda: (g1.at[:, c], g1r.at[j - 1], dev(x, lax.rem(y + j, NY), z, k)), ("gy", j))

    sum_x(2)
    acc = jnp.zeros((HIDT, FEAT), F32)
    for t in range(4):
        acc = acc + jnp.dot(gT[(t % 2) * 2 + t // 2], X[t], preferred_element_type=F32)
    g_in[...] = acc.astype(BF16)
    stores.append(pltpu.make_async_copy(g_in, gin_any, lsem.at[7]))
    stores[1].start()
    sum_x(1)
    for i in range(3):
        got(lambda: o1r.at[i], ("oy", i))
    o2[...] = (
        o1[:, :, cols(y)].astype(F32) + o1r[0].astype(F32) + o1r[1].astype(F32) + o1r[2].astype(F32)
    ).astype(BF16)
    for i, p in enumerate(zs):
        put(lambda: (o2.at[lax.div(p, NL), prow(lax.rem(p, NL))], o2r.at[i], dev(x, y, p, k)),
            ("oz", i))
    sum_x(3)
    sum_x(0)
    for j in (1, 2, 3):
        got(lambda: g1r.at[j - 1], ("gy", j))
    g2[...] = (
        g1[:, cols(y)].astype(F32) + g1r[0].astype(F32) + g1r[1].astype(F32) + g1r[2].astype(F32)
    ).astype(BF16)
    for d in range(NL):
        put(lambda: (g2.at[prow(ls[d])], g2r.at[1, d], dev(x, y, zp - zl + ls[d], k)),
            ("gzo", d), away)
        if d:
            put(lambda: (g2.at[prow(ls[d])], g2r.at[0, d], dev(x, y, zh * NL + ls[d], k)),
                ("gzs", d), home)
    mine = (prow(zl), cols(y))
    for i in range(NZ - 1):
        got(lambda: o2r.at[i], ("oz", i))
    piece = o2[zh, prow(zl), :].astype(F32)
    for i in range(NZ - 1):
        piece = piece + o2r[i].astype(F32)
    out[mine] = (x_ref[mine].astype(F32) + piece).astype(BF16)
    for d in range(1, NL):
        put(lambda: (out.at[mine], out.at[mine], dev(x, y, zh * NL + ls[d], k)), ("oal", d))

    @pl.when(home)
    def _():
        for d in range(NL):
            arrived(g2r.at[1, d], w.slot("gzo", d))
            if d:
                arrived(g2r.at[0, d], w.slot("gzs", d))
        same, other = g2[prow(zl), :].astype(F32), g2r[1, 0].astype(F32)
        for d in range(1, NL):
            same = same + g2r[0, d].astype(F32)
            other = other + g2r[1, d].astype(F32)
        gp[0] = same.astype(BF16)
        gp[1] = other.astype(BF16)

    for d in range(NL):
        for j in range(2):
            target = dev((zh if j == 0 else 1 - zh) * 2 + k, y, zh * NL + ls[d], kb)
            put(lambda: (gp.at[j], gn.at[mine], target), ("gal", d),
                beside_or_far(home, diag, d, j))

    @pl.when(diag)
    def _():
        gn[mine] = gp[0]

    from_l = [lax.rem(zl + NL - d, NL) for d in range(NL)]
    for d in range(1, NL):
        got(lambda: out.at[prow(from_l[d]), cols(y)], ("oal", d))
    for i, p in enumerate(ys):
        put(lambda: (out.at[:, cols(y)], out.at[:, cols(y)], dev(x, p, z, k)), ("oay", i))
    mean, rstd = st_ref[:, 0:1], st_ref[:, 1:2]
    scaled = (x_ref[...].astype(F32) - mean) * rstd
    g0[...] = scaled
    for d in range(NL):
        got(lambda: gn.at[prow(from_l[d]), cols(y)], ("gal", d), no(diag) if d == 0 else None)
    for i, p in enumerate(ys):
        put(lambda: (gn.at[:, cols(y)], gn.at[:, cols(y)], dev(x, p, z, k)), ("gay", i))
    gain_row = gain_cols(gain, y)
    gz = gn[:, cols(y)].astype(F32) * gain_row
    stats[0] = pack_pair(
        jnp.sum(gz, -1, keepdims=True), jnp.sum(gz * g0[:, cols(y)], -1, keepdims=True)
    )
    for dx in range(4):
        for dy in range(4):
            if dx or dy:
                put(lambda: (stats.at[0], stats.at[dx * 4 + dy],
                             dev(lax.rem(x + dx, NX), lax.rem(y + dy, NY), z, k)), ("ls", dx, dy))
    for i in range(3):
        got(lambda: out.at[:, cols(from_y[i])], ("oay", i))
    stores.append(pltpu.make_async_copy(out, out_any, lsem.at[8]))
    stores[2].start()
    for n in range(1, 16):
        got(lambda: stats.at[n], ("ls", n // 4, n % 4))
    sums_all = stats[0]
    for n in range(1, 16):
        sums_all = sums_all + stats[n]
    first, second = unpack_pair(sums_all)
    for i in range(3):
        got(lambda: gn.at[:, cols(from_y[i])], ("gay", i))
    gz = gn[...].astype(F32) * gain
    delta = rstd * (gz - first / D - g0[...] * (second / D))
    gx[...] = (cot_ref[...].astype(F32) + delta).astype(BF16)
    stores.append(pltpu.make_async_copy(gx, gx_any, lsem.at[9]))
    stores[3].start()
    w.finish()
    for store in stores:
        store.wait()
    assert len(w.sent) <= N_SEND and len(w.slots) <= N_RECV


def beside_or_far(home, diag, d, j):
    if d == 0 and j == 0:
        return jnp.logical_and(home, jnp.logical_not(diag))
    return home


def gain_cols(gain, y):
    part = gain[:, 0:PC]
    for i in range(1, NY):
        part = jnp.where(y == i, gain[:, i * PC:(i + 1) * PC], part)
    return part


def hand_kernel(a, b, c, d, ao, bo, co, do, sem):
    copies = [
        pltpu.make_async_copy(src, dst, sem.at[i])
        for i, (src, dst) in enumerate(((a, ao), (b, bo), (c, co), (d, do)))
    ]
    for copy in copies:
        copy.start()
    for copy in copies:
        copy.wait()


def per_device(inputs, cotangent, ln_gain, ln_bias, w_in, w_out):
    dma = pltpu.SemaphoreType.DMA
    tile = jax.ShapeDtypeStruct((TOK, FEAT), BF16)
    grad = jax.ShapeDtypeStruct((HIDT, FEAT), BF16)

    def vb(*shape):
        return pltpu.VMEM(shape, BF16)

    def vf(*shape):
        return pltpu.VMEM(shape, F32)

    results = pl.pallas_call(
        layer_kernel,
        name="layer",
        out_shape=[tile, tile, grad, grad],
        in_specs=[ANY] * 6,
        out_specs=[ANY] * 4,
        scratch_shapes=[
            vb(TOK, FEAT), vb(TOK, FEAT), vf(FEAT), vf(FEAT), vb(HIDT, FEAT), vb(HIDT, FEAT),
            vb(4, TOK, FEAT), vb(4, TOK, FEAT), vb(TOK, FEAT), vf(4, 8, TOK), vf(TOK, TOK),
            vf(4, HIDT, TOK), vf(2, HIDT, TOK), vb(2, HIDT, TOK), vb(2, HIDT, TOK),
            vb(3, HIDT, TOK), vb(3, HIDT, TOK), vb(HIDT, TOK), vb(2, HIDT, TOK),
            vb(4, HIDT, TOK), vb(4, HIDT, TOK), vb(4, TOK, HIDT), vb(2, HIDT, TOK),
            vb(3, TOK, FEAT), vb(3, TOK, FEAT), vf(TOK, FEAT), vb(TOK, FEAT), vb(3, TOK, PC),
            vb(TOK, PC), vb(2, NL, PR, PC), vb(2, PR, PC), vb(TOK, FEAT),
            vb(2, TOK, FEAT), vb(2, TOK, FEAT), vf(2, TOK, FEAT), vb(2, TOK, FEAT),
            vb(3, 2, TOK, PC), vb(2, TOK, PC), vb(NZ - 1, PR, PC), vf(16, 8, TOK),
            vb(TOK, FEAT), vb(TOK, FEAT), vb(HIDT, FEAT), vb(HIDT, FEAT),
            dma((N_SEND,)), dma((N_RECV,)), dma((10,)),
        ],
        compiler_params=pltpu.CompilerParams(
            collective_id=0, has_side_effects=True, vmem_limit_bytes=48 << 20
        ),
    )(inputs, cotangent, ln_gain, ln_bias, w_in.T, w_out)
    out, gx, g_in, g_out = pl.pallas_call(
        hand_kernel,
        name="hand",
        out_shape=[tile, tile, grad, grad],
        in_specs=[ANY] * 4,
        out_specs=[ANY] * 4,
        scratch_shapes=[dma((4,))],
    )(*results)
    return out, gx, g_in.T, g_out


def solution(mesh):
    return jax.shard_map(
        per_device,
        mesh=mesh,
        in_specs=(
            P("row", "col"),
            P("row", "col"),
            P("col"),
            P("col"),
            P("row", ("section", "col")),
            P(("section", "row"), "col"),
        ),
        out_specs=(
            P("row", "col"),
            P("row", "col"),
            P("row", ("section", "col")),
            P(("section", "row"), "col"),
        ),
        check_vma=False,
    )
```

```python
import jax
import jax.numpy as jnp
from jax import lax
from jax.experimental import pallas as pl
from jax.experimental.pallas import tpu as pltpu
from jax.sharding import PartitionSpec as P

EPS = 1e-05
SLOPE = 0.7978845608028654
CUBIC = 0.044715
F32, BF16 = jnp.float32, jnp.bfloat16
NX, NY, NZ, NL = 4, 4, 16, 8
TOK, FEAT, HIDT = 128, 1536, 192
D = NX * FEAT
QR = TOK // NY
PR, PC = TOK // NL, FEAT // NY
HBM = pl.BlockSpec(memory_space=pltpu.HBM)
NT = (((1,), (1,)), ((), ()))
TN = (((0,), (0,)), ((), ()))


def gelu_both(values):
    inner = jnp.tanh(SLOPE * (values + CUBIC * values * values * values))
    act = 0.5 * values * (1.0 + inner)
    slope = 0.5 * (1.0 + inner) + 0.5 * values * (1.0 - inner * inner) * SLOPE * (
        1.0 + 3.0 * CUBIC * values * values
    )
    return act, slope


def place():
    section, row, x = lax.axis_index("section"), lax.axis_index("row"), lax.axis_index("col")
    y, zl = lax.div(section, NL), lax.rem(section, NL)
    zh, k = lax.div(row, 2), lax.rem(row, 2)
    return x, y, zh * NL + zl, zh, zl, k, row


def dev(x, y, z, k):
    return (y * NL + lax.rem(z, NL), lax.div(z, NL) * 2 + k, x)

def al(value, mult):
    return pl.multiple_of(value, mult)


def pack_pair(first, second):
    lane = lax.broadcasted_iota(jnp.int32, (TOK, TOK), 1)
    both = jnp.where(lane == 0, first, jnp.where(lane == 1, second, 0.0))
    return both.T[0:8, :]


def unpack_pair(packed):
    both = jnp.concatenate([packed, jnp.zeros((TOK - 8, TOK), F32)], axis=0).T
    return both[:, 0:1], both[:, 1:2]


def arrived(ref, sem):
    pltpu.make_async_copy(ref, ref, sem).wait()


class Wires:
    def __init__(self, ssem, rsem):
        self.ssem, self.rsem = ssem, rsem
        self.slots, self.sent = {}, []

    def slot(self, *name):
        return self.rsem.at[self.slots.setdefault(name, len(self.slots))]

    def block(self, name, size):
        base = len(self.slots)
        for i in range(size):
            self.slot(name, i)
        return lambda i: self.rsem.at[base + i]

    def put(self, make, name, pred=None):
        rsem = self.slot(*name) if isinstance(name, tuple) else name
        ssem = self.ssem.at[len(self.sent)]

        src, dst, to = make()

        def copy():
            return pltpu.make_async_remote_copy(
                src_ref=src, dst_ref=dst, send_sem=ssem, recv_sem=rsem,
                device_id=to, device_id_type=pl.DeviceIdType.MESH,
            )

        when(pred, lambda: copy().start())
        self.sent.append((pred, copy))

    def got(self, make, name, pred=None):
        ref = make()
        sem = self.slot(*name) if isinstance(name, tuple) else name
        when(pred, lambda: arrived(ref, sem))

    def finish(self):
        for pred, copy in self.sent:
            when(pred, lambda copy=copy: copy().wait_send())


def when(pred, act):
    if pred is None:
        act()
    else:
        pl.when(pred)(act)


def both(*flags):
    result = flags[0]
    for flag in flags[1:]:
        result = jnp.logical_and(result, flag)
    return result


N_SEND, N_RECV = 190, 160


def layer_kernel(
    x_any, cot_any, gain_any, bias_any, win_any, wout_any,
    out_any, gx_any, gin_any, gout_any,
    x_ref, cot_ref, gain_ref, bias_ref, w_in, w_out,
    X, C, xn, sums, st_ref,
    hs, hr, us, ur, qs, qr, ts, tr, aT, at,
    WX, gA, g0, gq, g1r, g2, g2r, gp, gn, sc, stb,
    os, orr, o0, o1, o1r, o2, o2r, stats, out, gx, g_in, g_out,
    ssem, rsem, lsem,
):
    x, y, z, zh, zl, k, r = place()
    no = jnp.logical_not
    w = Wires(ssem, rsem)
    put, got = w.put, w.got
    loads = [
        pltpu.make_async_copy(src, dst, lsem.at[i])
        for i, (src, dst) in enumerate((
            (x_any, x_ref), (cot_any, cot_ref), (gain_any, gain_ref),
            (bias_any, bias_ref), (win_any, w_in), (wout_any, w_out),
        ))
    ]
    for load in loads:
        load.start()
    zm, zp = NZ - 1 - z, (1 - zh) * NL + zl
    par = lax.rem(zl, 2)
    zn = z + 1 - 2 * par
    xs = [lax.rem(x + d, NX) for d in (1, 2, 3)]
    ys = [lax.rem(y + d, NY) for d in (1, 2, 3)]
    zs = [lax.rem(z + d, NZ) for d in range(1, NZ)]
    ls = [lax.rem(zl + d, NL) for d in range(NL)]
    diag = r == x
    zb, kb = lax.div(x, 2), lax.rem(x, 2)
    home = zb == zh
    beside = jnp.logical_and(home, k != kb)
    core, pair = dev(x, y, z, 1 - k), dev(x, y, zp, k)
    zr, kt, ze = lax.div(zl, 4), lax.rem(lax.div(zl, 2), 2), lax.rem(zl, 2)
    owns = both(zr == zb, kt == k, k == kb)

    barrier = pltpu.get_barrier_semaphore()

    def greet(peer, pred=None):
        when(pred, lambda: pl.semaphore_signal(
            barrier, inc=1, device_id=peer, device_id_type=pl.DeviceIdType.MESH))

    for p in zs:
        greet(dev(x, y, p, k))
    greet(core)
    greet(dev(x, y, zm, 1 - k))
    for dx in range(4):
        for dy in range(4):
            if dx or dy:
                greet(dev(lax.rem(x + dx, NX), lax.rem(y + dy, NY), z, k))
    section = lax.axis_index("section")
    for half in range(2):
        greet((section, x, half * 2 + k), no(jnp.logical_and(diag, zh == half)))
    greet(dev(r, y, z, 1 - k), no(diag))
    for q in range(NX):
        for e in range(2):
            greet(dev(q, y, zh * NL + zb * 4 + k * 2 + e, kb),
                  no(both(owns, x == q, lax.rem(zl, 2) == e)))

    def num(flag):
        return flag.astype(jnp.int32)
    total = 15 + 2 + 15 + 2 - num(diag) + 3 * num(beside) + 8 - num(owns)

    loads[0].wait()
    rows = x_ref[...].astype(F32)
    sums[0] = pack_pair(
        jnp.sum(rows, -1, keepdims=True), jnp.sum(rows * rows, -1, keepdims=True)
    )
    loads[1].wait()
    loads[2].wait()
    loads[3].wait()
    pl.semaphore_wait(barrier, total)

    def rows_at(start, size):
        return pl.ds(al(start, 16), size)

    def cols(p):
        return pl.ds(al(p * PC, PC), PC)

    def prow(p):
        return pl.ds(al(p * PR, PR), PR)

    mine8 = rows_at(y * QR + par * 16, 16)
    theirs8 = rows_at(y * QR + (1 - par) * 16, 16)
    quarter = rows_at(y * QR, QR)
    front, back = (slice(None), pl.ds(0, PC)), (quarter, pl.ds(PC, FEAT - PC))
    tiles = [zh * 2 + k, zh * 2 + 1 - k, (1 - zh) * 2 + k, (1 - zh) * 2 + 1 - k]

    for i, p in enumerate(xs):
        put(lambda: (sums.at[0], sums.at[1 + i], dev(p, y, z, k)), ("stat", i))
    loads[4].wait()
    for i in (1, 0, 2):
        put(lambda: (w_in.at[:, cols(xs[i])], WX.at[x], dev(xs[i], y, z, k)), ("wx", i))
    WX[x] = w_in[:, cols(x)]
    put(lambda: (cot_ref.at[mine8], C.at[r, mine8], dev(x, y, zm, k)), ("cz",))
    put(lambda: (cot_ref, C.at[r], core), ("cc",))
    C[r] = cot_ref[...]
    for i in range(3):
        got(lambda: sums.at[1 + i], ("stat", i))
    first, second = unpack_pair((sums[0] + sums[1]) + (sums[2] + sums[3]))
    mean = first / D
    rstd = lax.rsqrt(second / D - mean * mean + EPS)
    lane = lax.broadcasted_iota(jnp.int32, (TOK, TOK), 1)
    st_ref[...] = jnp.where(lane == 0, mean, rstd)
    gain = gain_ref[...].reshape(1, FEAT)
    bias = bias_ref[...].reshape(1, FEAT)
    xn[...] = ((x_ref[...].astype(F32) - mean) * rstd * gain + bias).astype(BF16)

    away = no(home)
    for j in range(2):
        put(lambda: (xn.at[mine8], X.at[r, mine8], dev(x, y, zm, k if j == 0 else 1 - k)),
            ("xz", j), jnp.logical_and(away, (k == kb) if j == 0 else (k != kb)))
    put(lambda: (xn.at[back], X.at[(r, *back)], core), ("xb", 1), beside)
    put(lambda: (xn.at[front], X.at[(r, *front)], core), ("xf", 1), beside)

    @pl.when(diag)
    def _():
        X[(r, *back)] = xn[back]
        X[(r, *front)] = xn[front]

    def spread(ref, name):
        for i, p in enumerate(xs):
            put(lambda: (ref, ref, dev(p, y, z, k)), name, diag)

    def along_y(ref, name):
        for i, p in enumerate(ys):
            put(lambda: (ref, ref, dev(x, p, z, k)), name + (i,))

    for d in range(2):
        ref = X.at[(tiles[d], *back)]
        got(lambda: ref, ("xb", d), no(diag) if d == 0 else None)
        spread(ref, ("xb", d))
        along_y(ref, ("yb", d))
    spread(X.at[(tiles[0], *front)], ("xf", 0))
    got(lambda: X.at[(tiles[1], *front)], ("xf", 1), diag)
    spread(X.at[(tiles[1], *front)], ("xf", 1))
    got(lambda: C.at[tiles[2], theirs8], ("cz",))
    put(lambda: (C.at[tiles[2], theirs8], C.at[tiles[2], theirs8], dev(x, y, zn, k)), ("cn",))
    for d in (2, 3):
        ref = X.at[tiles[d], theirs8]
        got(lambda: ref, ("xz", d - 2), diag)
        put(lambda: (ref, ref, dev(x, y, zn, k)), ("xn", d), diag)
    got(lambda: C.at[tiles[2], mine8], ("cn",))
    along_y(C.at[tiles[2], quarter], ("cy",))
    for d in (2, 3):
        got(lambda: X.at[tiles[d], mine8], ("xn", d), diag)
        spread(X.at[tiles[d], quarter], ("xq", d))
    for d in (2, 3):
        ref = X.at[tiles[d], quarter]
        got(lambda: ref, ("xq", d), no(diag))
        along_y(ref, ("yq", d))
    from_y = [lax.rem(y + NY - 1 - i, NY) for i in range(3)]
    from_x = [lax.rem(x + NX - 1 - i, NX) for i in range(3)]

    loads[5].wait()
    for d in range(2):
        got(lambda: X.at[(tiles[d], *front)], ("xf", d), no(diag))
        for i in range(3):
            got(lambda: X.at[tiles[d], rows_at(from_y[i] * QR, QR), pl.ds(PC, FEAT - PC)], ("yb", d, i))

    def hid(t):
        return lax.dot_general(w_in[...], X[t], NT, preferred_element_type=F32)

    def grad(t):
        return lax.dot_general(w_out[...], C[t], NT, preferred_element_type=F32)

    hs[0] = hid(tiles[1])
    put(lambda: (hs.at[0], hr.at[0], core), ("hc", 0))
    near = hid(tiles[0])
    for i in range(3):
        got(lambda: C.at[tiles[2], rows_at(from_y[i] * QR, QR)], ("cy", i))
    put(lambda: (C.at[tiles[2]], C.at[tiles[2]], core), ("cf",))
    got(lambda: hr.at[0], ("hc", 0))
    h_near = near + hr[0]
    us[0] = h_near.astype(BF16)
    put(lambda: (us.at[0], ur.at[1], pair), ("hz", 0))
    hs[2] = h_near
    got(lambda: C.at[tiles[1]], ("cc",))
    got(lambda: C.at[tiles[3]], ("cf",))
    for i in (1, 0, 2):
        qs[i] = grad(xs[i]).astype(BF16)
        put(lambda: (qs.at[i], qr.at[i], dev(xs[i], y, z, k)), ("ga", i))
    own = grad(x)
    for i in range(3):
        got(lambda: qr.at[i], ("ga", i))
    ts[...] = (own + qr[0].astype(F32) + qr[1].astype(F32) + qr[2].astype(F32)).astype(BF16)
    for half in range(2):
        selfish = jnp.logical_and(diag, zh == half)
        for side in range(2):
            put(lambda: (ts, tr.at[side], (section, half * 2 + kb, r)), ("gt", side),
                jnp.logical_and(no(selfish), zb == side))

    @pl.when(diag)
    def _():
        tr[zh] = ts[...]

    for d in (2, 3):
        for i in range(3):
            got(lambda: X.at[tiles[d], rows_at(from_y[i] * QR, QR)], ("yq", d, i))
    hs[1] = hid(tiles[3])
    put(lambda: (hs.at[1], hr.at[1], core), ("hc", 1))
    far = hid(tiles[2])
    got(lambda: hr.at[1], ("hc", 1))
    h_far = far + hr[1]
    us[1] = h_far.astype(BF16)
    put(lambda: (us.at[1], ur.at[0], pair), ("hz", 1))
    hs[3] = h_far
    for side in range(2):
        got(lambda: tr.at[side], ("gt", side), no(jnp.logical_and(diag, zh == side)))

    def activate(step, half):
        act, slope = gelu_both(hs[2 + step] + ur[step].astype(F32))
        gA[k * 2 + half, x] = (tr[half].astype(F32) * slope).astype(BF16)
        at[half] = act.astype(BF16)

    def spread_gh(step, pos):
        ref = gA.at[pos, x]
        for i in (1, 0, 2):
            put(lambda: (ref, ref, dev(xs[i], y, z, k)), ("gg", step, i))
        put(lambda: (ref, ref, core), ("gc", step))

    got(lambda: ur.at[1], ("hz", 0))
    activate(1, 1 - zh)
    spread_gh(1, k * 2 + 1 - zh)
    got(lambda: ur.at[0], ("hz", 1))
    activate(0, zh)
    spread_gh(0, k * 2 + zh)
    held = pl.ds(k * 2, 2)
    for i, p in enumerate(xs):
        put(lambda: (at, aT.at[held], dev(p, y, z, k)), ("ax", 0), diag)
    for i, p in enumerate(xs):
        put(lambda: (at, aT.at[held], dev(p, y, z, 1 - k)), ("ax", 1), beside)
    put(lambda: (at, aT.at[held], core), ("ax", 1), beside)

    @pl.when(diag)
    def _():
        aT[held] = at[...]

    unheld = pl.ds((1 - k) * 2, 2)
    for i in (0, 2, 1):
        for step, pos in ((1, k * 2 + 1 - zh), (0, k * 2 + zh)):
            got(lambda: gA.at[pos, from_x[i]], ("gg", step, i))
        put(lambda: (gA.at[held, from_x[i]], gA.at[held, from_x[i]], core), ("gf", i))
    for i in range(3):
        got(lambda: WX.at[from_x[i]], ("wx", i))
    got(lambda: gA.at[(1 - k) * 2 + 1 - zh, x], ("gc", 1))
    got(lambda: gA.at[(1 - k) * 2 + zh, x], ("gc", 0))
    for i in (0, 2, 1):
        got(lambda: gA.at[unheld, from_x[i]], ("gf", i))

    slab = WX[...].reshape(NX * HIDT, PC)
    for p in range(4):
        g0[p] = lax.dot_general(
            gA[p].reshape(NX * HIDT, TOK), slab, TN, preferred_element_type=F32)
    gq[...] = g0[...].astype(BF16)
    for i in (1, 0, 2):
        put(lambda: (gq.at[:, rows_at(ys[i] * QR, QR)], g1r.at[i], dev(x, ys[i], z, k)), ("gy", i))

    got(lambda: aT.at[held], ("ax", 0), no(diag))
    got(lambda: aT.at[unheld], ("ax", 1))
    halves = (1 - zh, zh)

    def part_o(pos):
        return lax.dot_general(aT[pos], w_out[...], TN, preferred_element_type=F32)

    for c in range(2):
        os[c] = part_o((1 - k) * 2 + halves[c]).astype(BF16)
        put(lambda: (os.at[c], orr.at[c], core), ("oc", c))
    for c in range(2):
        o0[c] = part_o(k * 2 + halves[c])
    for c in range(2):
        got(lambda: orr.at[c], ("oc", c))
        o1[c] = (o0[c] + orr[c].astype(F32)).astype(BF16)
        for i in (1, 0, 2):
            put(lambda: (o1.at[c, :, cols(ys[i])], o1r.at[c, i], dev(x, ys[i], z, k)), ("oy", c, i))

    def weight_grad(left, right):
        acc = jnp.dot(left(0), right[0], preferred_element_type=F32)
        for t in range(1, 4):
            acc = acc + jnp.dot(left((t % 2) * 2 + t // 2), right[t], preferred_element_type=F32)
        return acc.astype(BF16)

    g_out[...] = weight_grad(lambda p: aT[p], C)
    stores = [pltpu.make_async_copy(g_out, gout_any, lsem.at[6])]
    stores[0].start()

    for i in range(3):
        got(lambda: g1r.at[i], ("gy", i))
    g2[...] = (
        g0[:, quarter, :] + g1r[0].astype(F32) + g1r[1].astype(F32) + g1r[2].astype(F32)
    ).astype(BF16)
    zsem = w.block("gz", NL)
    for p in range(4):
        for e in range(2):
            target = (p % 2) * NL + zh * 4 + (p // 2) * 2 + e
            put(lambda: (g2.at[p, pl.ds(e * 16, 16)], g2r.at[zl], dev(x, y, target, k)),
                zsem(zl), z != target)
    mine_here = zr == zh

    @pl.when(mine_here)
    def _():
        g2r[zl] = g2[kt * 2 + zh, rows_at(ze * 16, 16), :]

    g_in[...] = weight_grad(lambda p: gA[p, x], X)
    stores.append(pltpu.make_async_copy(g_in, gin_any, lsem.at[7]))
    stores[1].start()

    for c in range(2):
        for i in range(3):
            got(lambda: o1r.at[c, i], ("oy", c, i))
        o2[c] = (
            o1[c, :, cols(y)].astype(F32) + o1r[c, 0].astype(F32)
            + o1r[c, 1].astype(F32) + o1r[c, 2].astype(F32)
        ).astype(BF16)
        for d in range(c, NL):
            target = halves[c] * NL + ls[d]
            put(lambda: (o2.at[c, prow(ls[d])], o2r.at[c, d], dev(x, y, target, k)), ("oz", c, d))

    for n in range(NL):
        got(lambda: g2r.at[n], zsem(n), no(both(mine_here, zl == n)))
    piece = g2r[0].astype(F32)
    for n in range(1, NL):
        piece = piece + g2r[n].astype(F32)
    gp[...] = piece.astype(BF16)
    asem = w.block("gal", NX * 2)
    here = (rows_at(y * QR + ze * 16, 16), cols(x))
    for d in range(NL):
        put(lambda: (gp, gn.at[here], dev(zr * 2 + k, y, zh * NL + ls[d], kt)),
            asem(x * 2 + ze), no(owns) if d == 0 else None)

    @pl.when(owns)
    def _():
        gn[here] = gp[...]

    mine = (prow(zl), cols(y))
    for c in range(2):
        for d in range(c, NL):
            got(lambda: o2r.at[c, d], ("oz", c, d))
    piece = o2[1, prow(zl), :].astype(F32)
    for c in range(2):
        for d in range(c, NL):
            piece = piece + o2r[c, d].astype(F32)
    out[mine] = (x_ref[mine].astype(F32) + piece).astype(BF16)
    for d in range(1, NL):
        put(lambda: (out.at[mine], out.at[mine], dev(x, y, zh * NL + ls[d], k)), ("oal", d))

    mean, rstd = st_ref[:, 0:1], st_ref[:, 1:2]
    sc[...] = (x_ref[...].astype(F32) - mean) * rstd
    stb[...] = jnp.zeros((TOK, TOK), F32)
    for q in range(NX):
        for e in range(2):
            got(lambda: gn.at[rows_at(y * QR + e * 16, 16), pl.ds(q * PC, PC)], asem(q * 2 + e),
                no(both(owns, x == q, ze == e)))
    for i in (1, 0, 2):
        put(lambda: (gn.at[quarter], gn.at[quarter], dev(x, ys[i], z, k)), ("gay", i))
    gz = gn[quarter, :].astype(F32) * gain
    lane = lax.broadcasted_iota(jnp.int32, (QR, TOK), 1)
    first = jnp.sum(gz, -1, keepdims=True)
    second = jnp.sum(gz * sc[quarter, :], -1, keepdims=True)
    stb[quarter, :] = jnp.where(lane == 0, first, jnp.where(lane == 1, second, 0.0))
    stats[0] = stb[...].T[0:8, :]
    for dx in range(4):
        for dy in range(4):
            if dx or dy:
                put(lambda: (stats.at[0], stats.at[dx * 4 + dy],
                             dev(lax.rem(x + dx, NX), lax.rem(y + dy, NY), z, k)), ("ls", dx, dy))
    from_l = [lax.rem(zl + NL - d, NL) for d in range(NL)]
    for d in range(1, NL):
        got(lambda: out.at[prow(from_l[d]), cols(y)], ("oal", d))
    for i in (1, 0, 2):
        put(lambda: (out.at[:, cols(y)], out.at[:, cols(y)], dev(x, ys[i], z, k)), ("oay", i))
    for n in range(1, 16):
        got(lambda: stats.at[n], ("ls", n // 4, n % 4))
    sums_all = stats[0]
    for n in range(1, 16):
        sums_all = sums_all + stats[n]
    first, second = unpack_pair(sums_all)
    for i in range(3):
        got(lambda: gn.at[rows_at(from_y[i] * QR, QR)], ("gay", i))
    gz = gn[...].astype(F32) * gain
    delta = rstd * (gz - first / D - sc[...] * (second / D))
    gx[...] = (cot_ref[...].astype(F32) + delta).astype(BF16)
    stores.append(pltpu.make_async_copy(gx, gx_any, lsem.at[9]))
    stores[2].start()
    for i in range(3):
        got(lambda: out.at[:, cols(from_y[i])], ("oay", i))
    stores.append(pltpu.make_async_copy(out, out_any, lsem.at[8]))
    stores[3].start()
    w.finish()
    for store in stores:
        store.wait()
    assert len(w.sent) <= N_SEND and len(w.slots) <= N_RECV


def per_device(inputs, cotangent, ln_gain, ln_bias, w_in, w_out):
    dma = pltpu.SemaphoreType.DMA
    tile = jax.ShapeDtypeStruct((TOK, FEAT), BF16)
    grad = jax.ShapeDtypeStruct((HIDT, FEAT), BF16)

    def vb(*shape):
        return pltpu.VMEM(shape, BF16)

    def vf(*shape):
        return pltpu.VMEM(shape, F32)

    out, gx, g_in, g_out = pl.pallas_call(
        layer_kernel,
        name="layer",
        out_shape=[tile, tile, grad, grad],
        in_specs=[HBM] * 6,
        out_specs=[HBM] * 4,
        scratch_shapes=[
            vb(TOK, FEAT), vb(TOK, FEAT), vf(FEAT), vf(FEAT), vb(HIDT, FEAT), vb(HIDT, FEAT),
            vb(4, TOK, FEAT), vb(4, TOK, FEAT), vb(TOK, FEAT), vf(4, 8, TOK), vf(TOK, TOK),
            vf(4, HIDT, TOK), vf(2, HIDT, TOK), vb(2, HIDT, TOK), vb(2, HIDT, TOK),
            vb(3, HIDT, TOK), vb(3, HIDT, TOK), vb(HIDT, TOK), vb(2, HIDT, TOK),
            vb(4, HIDT, TOK), vb(2, HIDT, TOK),
            vb(NX, HIDT, PC), vb(4, NX, HIDT, TOK), vf(4, TOK, PC), vb(4, TOK, PC), vb(3, 4, QR, PC),
            vb(4, QR, PC), vb(NL, PR, PC), vb(PR, PC), vb(TOK, FEAT), vf(TOK, FEAT), vf(TOK, TOK),
            vb(2, TOK, FEAT), vb(2, TOK, FEAT), vf(2, TOK, FEAT), vb(2, TOK, FEAT),
            vb(2, 3, TOK, PC), vb(2, TOK, PC), vb(2, NL, PR, PC), vf(16, 8, TOK),
            vb(TOK, FEAT), vb(TOK, FEAT), vb(HIDT, FEAT), vb(HIDT, FEAT),
            dma((N_SEND,)), dma((N_RECV,)), dma((10,)),
        ],
        compiler_params=pltpu.CompilerParams(
            collective_id=0, has_side_effects=True, vmem_limit_bytes=63 << 20
        ),
    )(inputs, cotangent, ln_gain, ln_bias, w_in.T, w_out)
    return out, gx, g_in.T, g_out


def solution(mesh):
    return jax.shard_map(
        per_device,
        mesh=mesh,
        in_specs=(
            P("row", "col"),
            P("row", "col"),
            P("col"),
            P("col"),
            P("row", ("section", "col")),
            P(("section", "row"), "col"),
        ),
        out_specs=(
            P("row", "col"),
            P("row", "col"),
            P("row", ("section", "col")),
            P(("section", "row"), "col"),
        ),
        check_vma=False,
    )
```

```python
import jax
import jax.numpy as jnp
from jax import lax
from jax.experimental import pallas as pl
from jax.experimental.pallas import tpu as pltpu
from jax.sharding import PartitionSpec as P

EPS = 1e-05
SLOPE = 0.7978845608028654
CUBIC = 0.044715
F32, BF16 = jnp.float32, jnp.bfloat16
NX, NY, NZ, NL = 4, 4, 16, 8
TOK, FEAT, HIDT = 128, 1536, 192
D = NX * FEAT
QR = TOK // NY
PR, PC = TOK // NL, FEAT // NY
VMEM = pl.BlockSpec(memory_space=pltpu.VMEM)
HBM = pl.BlockSpec(memory_space=pltpu.HBM)
NT = (((1,), (1,)), ((), ()))
TN = (((0,), (0,)), ((), ()))


def gelu_both(values):
    inner = jnp.tanh(SLOPE * (values + CUBIC * values * values * values))
    act = 0.5 * values * (1.0 + inner)
    slope = 0.5 * (1.0 + inner) + 0.5 * values * (1.0 - inner * inner) * SLOPE * (
        1.0 + 3.0 * CUBIC * values * values
    )
    return act, slope


def place():
    section, row, x = lax.axis_index("section"), lax.axis_index("row"), lax.axis_index("col")
    y, zl = lax.div(section, NL), lax.rem(section, NL)
    zh, k = lax.div(row, 2), lax.rem(row, 2)
    return x, y, zh * NL + zl, zh, zl, k, row


def dev(x, y, z, k):
    return (y * NL + lax.rem(z, NL), lax.div(z, NL) * 2 + k, x)

def al(value, mult):
    return pl.multiple_of(value, mult)


def pack_pair(first, second):
    lane = lax.broadcasted_iota(jnp.int32, (TOK, TOK), 1)
    both = jnp.where(lane == 0, first, jnp.where(lane == 1, second, 0.0))
    return both.T[0:8, :]


def unpack_pair(packed):
    both = jnp.concatenate([packed, jnp.zeros((TOK - 8, TOK), F32)], axis=0).T
    return both[:, 0:1], both[:, 1:2]


def arrived(ref, sem):
    pltpu.make_async_copy(ref, ref, sem).wait()


class Wires:
    def __init__(self, ssem, rsem):
        self.ssem, self.rsem = ssem, rsem
        self.slots, self.sent = {}, []

    def slot(self, *name):
        return self.rsem.at[self.slots.setdefault(name, len(self.slots))]

    def block(self, name, size):
        base = len(self.slots)
        for i in range(size):
            self.slot(name, i)
        return lambda i: self.rsem.at[base + i]

    def put(self, make, name, pred=None):
        rsem = self.slot(*name) if isinstance(name, tuple) else name
        ssem = self.ssem.at[len(self.sent)]

        src, dst, to = make()

        def copy():
            return pltpu.make_async_remote_copy(
                src_ref=src, dst_ref=dst, send_sem=ssem, recv_sem=rsem,
                device_id=to, device_id_type=pl.DeviceIdType.MESH,
            )

        when(pred, lambda: copy().start())
        self.sent.append((pred, copy))

    def got(self, make, name, pred=None):
        ref = make()
        sem = self.slot(*name) if isinstance(name, tuple) else name
        when(pred, lambda: arrived(ref, sem))

    def finish(self):
        for pred, copy in self.sent:
            when(pred, lambda copy=copy: copy().wait_send())


def when(pred, act):
    if pred is None:
        act()
    else:
        pl.when(pred)(act)


def both(*flags):
    result = flags[0]
    for flag in flags[1:]:
        result = jnp.logical_and(result, flag)
    return result


N_SEND, N_RECV = 190, 160


def layer_kernel(
    x_any, cot_any, gain_any, bias_any, win_any, wout_any,
    out_any, gx_any, gin_any, gout_any,
    x_ref, cot_ref, gain_ref, bias_ref, w_in, w_out,
    X, C, N, sums, pairs, gb, st_ref,
    hs, hr, us, ur, qs, qr, ts, tr, aT, at,
    WX, gA, g0, gq, g1r, g2, g2r, gp, gn, sc, stb,
    os, orr, o0, o1, o1r, o2, o2r, stats, out, gx, g_in, g_out,
    ssem, rsem, lsem,
):
    x, y, z, zh, zl, k, r = place()
    no = jnp.logical_not
    w = Wires(ssem, rsem)
    put, got = w.put, w.got
    loads = [
        pltpu.make_async_copy(src, dst, lsem.at[i])
        for i, (src, dst) in enumerate((
            (x_any, x_ref), (cot_any, cot_ref), (gain_any, gain_ref),
            (bias_any, bias_ref), (win_any, w_in), (wout_any, w_out),
        ))
    ]
    for load in loads:
        load.start()
    zm, zp = NZ - 1 - z, (1 - zh) * NL + zl
    par = lax.rem(zl, 2)
    zn = z + 1 - 2 * par
    xs = [lax.rem(x + d, NX) for d in (1, 2, 3)]
    ys = [lax.rem(y + d, NY) for d in (1, 2, 3)]
    zs = [lax.rem(z + d, NZ) for d in range(1, NZ)]
    ls = [lax.rem(zl + d, NL) for d in range(NL)]
    diag = r == x
    zb, kb = lax.div(x, 2), lax.rem(x, 2)
    home = zb == zh
    beside = jnp.logical_and(home, k != kb)
    core, pair = dev(x, y, z, 1 - k), dev(x, y, zp, k)
    zr, kt, ze = lax.div(zl, 4), lax.rem(lax.div(zl, 2), 2), lax.rem(zl, 2)
    owns = both(zr == zb, kt == k, k == kb)

    barrier = pltpu.get_barrier_semaphore()

    def greet(peer, pred=None):
        when(pred, lambda: pl.semaphore_signal(
            barrier, inc=1, device_id=peer, device_id_type=pl.DeviceIdType.MESH))

    for p in zs:
        greet(dev(x, y, p, k))
    greet(core)
    greet(dev(x, y, zm, 1 - k))
    for dx in range(4):
        for dy in range(4):
            if dx or dy:
                greet(dev(lax.rem(x + dx, NX), lax.rem(y + dy, NY), z, k))
    section = lax.axis_index("section")
    for half in range(2):
        greet((section, x, half * 2 + k), no(jnp.logical_and(diag, zh == half)))
    greet(dev(r, y, z, 1 - k), no(diag))
    for q in range(NX):
        for e in range(2):
            greet(dev(q, y, zh * NL + zb * 4 + k * 2 + e, kb),
                  no(both(owns, x == q, lax.rem(zl, 2) == e)))

    def num(flag):
        return flag.astype(jnp.int32)
    total = 15 + 2 + 15 + 2 - num(diag) + 3 * num(beside) + 8 - num(owns)

    loads[0].wait()
    rows = x_ref[...].astype(F32)
    sums[0] = pack_pair(
        jnp.sum(rows, -1, keepdims=True), jnp.sum(rows * rows, -1, keepdims=True)
    )
    loads[1].wait()
    loads[2].wait()
    loads[3].wait()
    pl.semaphore_wait(barrier, total)

    def rows_at(start, size):
        return pl.ds(al(start, 16), size)

    def cols(p):
        return pl.ds(al(p * PC, PC), PC)

    def prow(p):
        return pl.ds(al(p * PR, PR), PR)

    mine8 = rows_at(y * QR + par * 16, 16)
    theirs8 = rows_at(y * QR + (1 - par) * 16, 16)
    quarter = rows_at(y * QR, QR)
    front, back = (slice(None), pl.ds(0, PC)), (quarter, pl.ds(PC, FEAT - PC))
    tiles = [zh * 2 + k, zh * 2 + 1 - k, (1 - zh) * 2 + k, (1 - zh) * 2 + 1 - k]

    def spread_x(ref, name):
        for i in (1, 0, 2):
            put(lambda: (ref, ref, dev(xs[i], y, z, k)), name, diag)

    def along_y(ref, name):
        for i in (1, 0, 2):
            put(lambda: (ref, ref, dev(x, ys[i], z, k)), name + (i,))

    from_y = [lax.rem(y + NY - 1 - i, NY) for i in range(3)]
    from_x = [lax.rem(x + NX - 1 - i, NX) for i in range(3)]
    away = no(home)

    for i, p in enumerate(xs):
        put(lambda: (sums.at[0], sums.at[1 + i], dev(p, y, z, k)), ("stat", i))
    for j in range(2):
        put(lambda: (x_ref.at[mine8], X.at[r, mine8], dev(x, y, zm, k if j == 0 else 1 - k)),
            ("xz", j), jnp.logical_and(away, (k == kb) if j == 0 else (k != kb)))
    put(lambda: (x_ref.at[back], X.at[(r, *back)], core), ("xb", 1), beside)
    put(lambda: (x_ref.at[front], X.at[(r, *front)], core), ("xf", 1), beside)
    put(lambda: (cot_ref, C.at[r], core), ("cc",))

    @pl.when(diag)
    def _():
        X[(r, *back)] = x_ref[back]
        X[(r, *front)] = x_ref[front]

    for d in range(2):
        ref = X.at[(tiles[d], *back)]
        if d:
            got(lambda: ref, ("xb", d), diag)
        spread_x(ref, ("xb", d))
    gain = gain_ref[...].reshape(1, FEAT)
    bias = bias_ref[...].reshape(1, FEAT)

    @pl.when(diag)
    def _():
        gb[0:1, :] = gain
        gb[1:2, :] = bias

    spread_x(gb, ("gb",))
    spread_x(X.at[(tiles[0], *front)], ("xf", 0))
    got(lambda: X.at[(tiles[1], *front)], ("xf", 1), diag)
    spread_x(X.at[(tiles[1], *front)], ("xf", 1))
    C[r] = cot_ref[...]
    for i in range(3):
        got(lambda: sums.at[1 + i], ("stat", i))
    pairs[0] = (sums[0] + sums[1]) + (sums[2] + sums[3])
    for d, to in ((2, dev(x, y, zm, k)), (3, dev(x, y, zm, 1 - k)), (1, core)):
        put(lambda: (pairs.at[0], pairs.at[d], to), ("pair", d))
    put(lambda: (cot_ref.at[mine8], C.at[r, mine8], dev(x, y, zm, k)), ("cz",))

    def moments(d):
        first, second = unpack_pair(pairs[d])
        mean = first / D
        return mean, lax.rsqrt(second / D - mean * mean + EPS)

    mean, rstd = moments(0)
    lane = lax.broadcasted_iota(jnp.int32, (TOK, TOK), 1)
    st_ref[...] = jnp.where(lane == 0, mean, rstd)
    for d in range(2):
        ref = X.at[(tiles[d], *back)]
        got(lambda: ref, ("xb", d), no(diag))
        along_y(ref, ("yb", d))
    two, three = X.at[tiles[2], theirs8], X.at[tiles[3], theirs8]
    got(lambda: two, ("xz", 0), diag)
    put(lambda: (two, two, dev(x, y, zn, k)), ("xn",), diag)
    got(lambda: three, ("xz", 1), diag)
    spread_x(three, ("xe",))
    got(lambda: X.at[tiles[2], mine8], ("xn",), diag)
    spread_x(X.at[tiles[2], quarter], ("xq",))
    got(lambda: C.at[tiles[2], theirs8], ("cz",))
    other = C.at[tiles[2], theirs8]
    along_y(other, ("cy",))
    put(lambda: (other, other, dev(x, y, zn, k)), ("ce", 3))
    got(lambda: three, ("xe",), no(diag))
    along_y(three, ("ye",))
    put(lambda: (three, three, dev(x, y, zn, k)), ("ze", 3))
    got(lambda: X.at[tiles[2], quarter], ("xq",), no(diag))
    along_y(X.at[tiles[2], quarter], ("yq",))
    loads[4].wait()
    for i in (1, 0, 2):
        put(lambda: (w_in.at[:, cols(xs[i])], WX.at[x], dev(xs[i], y, z, k)), ("wx", i))
    WX[x] = w_in[:, cols(x)]
    got(lambda: gb, ("gb",), no(diag))

    def normalize(d):
        if d:
            got(lambda: pairs.at[d], ("pair", d))
        mean, rstd = moments(d)
        N[tiles[d]] = (
            (X[tiles[d]].astype(F32) - mean) * rstd * gb[0:1, :] + gb[1:2, :]
        ).astype(BF16)

    loads[5].wait()
    for d in range(2):
        got(lambda: X.at[(tiles[d], *front)], ("xf", d), no(diag))
        for i in range(3):
            got(lambda: X.at[tiles[d], rows_at(from_y[i] * QR, QR), pl.ds(PC, FEAT - PC)], ("yb", d, i))
        normalize(d)

    def pass_eighths(tile, arrive, leave):
        for i in range(3):
            ref = tile.at[rows_at(from_y[i] * QR + (1 - par) * 16, 16)]
            got(lambda: ref, (arrive, i))
            put(lambda: (ref, ref, dev(x, y, zn, k)), (leave, i))

    def take_eighths(tile, arrive):
        got(lambda: tile.at[mine8], (arrive, 3))
        for i in range(3):
            got(lambda: tile.at[rows_at(from_y[i] * QR + par * 16, 16)], (arrive, i))

    def hid(t):
        return lax.dot_general(w_in[...], N[t], NT, preferred_element_type=F32)

    def grad(t):
        return lax.dot_general(w_out[...], C[t], NT, preferred_element_type=F32)

    hs[0] = hid(tiles[1])
    put(lambda: (hs.at[0], hr.at[0], core), ("hc", 0))
    near = hid(tiles[0])
    pass_eighths(C.at[tiles[2]], "cy", "ce")
    pass_eighths(X.at[tiles[3]], "ye", "ze")
    got(lambda: hr.at[0], ("hc", 0))
    h_near = near + hr[0]
    us[0] = h_near.astype(BF16)
    put(lambda: (us.at[0], ur.at[1], pair), ("hz", 0))
    hs[2] = h_near
    take_eighths(C.at[tiles[2]], "ce")
    put(lambda: (C.at[tiles[2]], C.at[tiles[2]], core), ("cf",))
    got(lambda: C.at[tiles[1]], ("cc",))
    got(lambda: C.at[tiles[3]], ("cf",))
    for i in (1, 0, 2):
        qs[i] = grad(xs[i]).astype(BF16)
        put(lambda: (qs.at[i], qr.at[i], dev(xs[i], y, z, k)), ("ga", i))
    own = grad(x)
    for i in range(3):
        got(lambda: X.at[tiles[2], rows_at(from_y[i] * QR, QR)], ("yq", i))
    normalize(2)
    far = hid(tiles[2])
    take_eighths(X.at[tiles[3]], "ze")
    normalize(3)
    hs[1] = hid(tiles[3])
    put(lambda: (hs.at[1], hr.at[1], core), ("hc", 1))
    for i in range(3):
        got(lambda: qr.at[i], ("ga", i))
    ts[...] = (own + qr[0].astype(F32) + qr[1].astype(F32) + qr[2].astype(F32)).astype(BF16)
    for half in range(2):
        selfish = jnp.logical_and(diag, zh == half)
        for side in range(2):
            put(lambda: (ts, tr.at[side], (section, half * 2 + kb, r)), ("gt", side),
                jnp.logical_and(no(selfish), zb == side))

    @pl.when(diag)
    def _():
        tr[zh] = ts[...]

    got(lambda: hr.at[1], ("hc", 1))
    h_far = far + hr[1]
    us[1] = h_far.astype(BF16)
    put(lambda: (us.at[1], ur.at[0], pair), ("hz", 1))
    hs[3] = h_far
    for side in range(2):
        got(lambda: tr.at[side], ("gt", side), no(jnp.logical_and(diag, zh == side)))

    def activate(step, half):
        act, slope = gelu_both(hs[2 + step] + ur[step].astype(F32))
        gA[k * 2 + half, x] = (tr[half].astype(F32) * slope).astype(BF16)
        at[half] = act.astype(BF16)

    def spread(step, half):
        for i, p in enumerate(xs):
            put(lambda: (at.at[half], aT.at[k * 2 + half], dev(p, y, z, k)), ("ax", 0, step), diag)
        for i, p in enumerate(xs):
            put(lambda: (at.at[half], aT.at[k * 2 + half], dev(p, y, z, 1 - k)),
                ("ax", 1, step), beside)
        put(lambda: (at.at[half], aT.at[k * 2 + half], core), ("ax", 1, step), beside)

        @pl.when(diag)
        def _():
            aT[k * 2 + half] = at[half]

        ref = gA.at[k * 2 + half, x]
        for i in (1, 0, 2):
            put(lambda: (ref, ref, dev(xs[i], y, z, k)), ("gg", step, i))
        put(lambda: (ref, ref, core), ("gc", step))

    def part_o(pos):
        return lax.dot_general(aT[pos], w_out[...], TN, preferred_element_type=F32)

    halves = (1 - zh, zh)

    def outputs(c):
        step, half = 1 - c, halves[c]
        held, unheld = k * 2 + half, (1 - k) * 2 + half
        got(lambda: aT.at[held], ("ax", 0, step), no(diag))
        got(lambda: aT.at[unheld], ("ax", 1, step))
        os[c] = part_o(unheld).astype(BF16)
        put(lambda: (os.at[c], orr.at[c], core), ("oc", c))
        o0[c] = part_o(held)
        for i in (0, 2, 1):
            ref = gA.at[held, from_x[i]]
            got(lambda: ref, ("gg", step, i))
            put(lambda: (ref, ref, core), ("gf", step, i))
        got(lambda: orr.at[c], ("oc", c))
        o1[c] = (o0[c] + orr[c].astype(F32)).astype(BF16)
        for i in (1, 0, 2):
            put(lambda: (o1.at[c, :, cols(ys[i])], o1r.at[c, i], dev(x, ys[i], z, k)), ("oy", c, i))
    def features(c):
        step, half = 1 - c, halves[c]
        unheld = (1 - k) * 2 + half
        if c == 0:
            for i in range(3):
                got(lambda: WX.at[from_x[i]], ("wx", i))
        got(lambda: gA.at[unheld, x], ("gc", step))
        for i in (0, 2, 1):
            got(lambda: gA.at[unheld, from_x[i]], ("gf", step, i))
        slab = WX[...].reshape(NX * HIDT, PC)
        for j in range(2):
            g0[c, j] = lax.dot_general(
                gA[j * 2 + half].reshape(NX * HIDT, TOK), slab, TN, preferred_element_type=F32)
        gq[c] = g0[c].astype(BF16)
        for i in (1, 0, 2):
            put(lambda: (gq.at[c, :, rows_at(ys[i] * QR, QR)], g1r.at[c, i],
                         dev(x, ys[i], z, k)), ("gy", c, i))

    zsem = w.block("gz", NL)

    def sums_y(c):
        for i in range(3):
            got(lambda: o1r.at[c, i], ("oy", c, i))
        o2[c] = (
            o1[c, :, cols(y)].astype(F32) + o1r[c, 0].astype(F32)
            + o1r[c, 1].astype(F32) + o1r[c, 2].astype(F32)
        ).astype(BF16)
        for d in range(c, NL):
            target = halves[c] * NL + ls[d]
            put(lambda: (o2.at[c, prow(ls[d])], o2r.at[c, d], dev(x, y, target, k)), ("oz", c, d))

    def feature_sums(c):
        for i in range(3):
            got(lambda: g1r.at[c, i], ("gy", c, i))
        g2[c] = (
            g0[c, :, quarter, :] + g1r[c, 0].astype(F32)
            + g1r[c, 1].astype(F32) + g1r[c, 2].astype(F32)
        ).astype(BF16)
        for j in range(2):
            for e in range(2):
                target = halves[c] * NL + zh * 4 + j * 2 + e
                put(lambda: (g2.at[c, j, pl.ds(e * 16, 16)], g2r.at[zl], dev(x, y, target, k)),
                    zsem(zl), (z != target) if c else None)

    got(lambda: ur.at[1], ("hz", 0))
    activate(1, 1 - zh)
    spread(1, 1 - zh)
    got(lambda: ur.at[0], ("hz", 1))
    activate(0, zh)
    spread(0, zh)
    outputs(0)
    outputs(1)
    features(0)
    features(1)
    sums_y(0)
    sums_y(1)
    feature_sums(0)

    def weight_grad(left, right):
        wide = jnp.concatenate([left((t % 2) * 2 + t // 2) for t in range(4)], axis=1)
        tall = right[...].reshape(4 * TOK, FEAT)
        return jnp.dot(wide, tall, preferred_element_type=F32).astype(BF16)

    g_out[...] = weight_grad(lambda p: aT[p], C)
    stores = [pltpu.make_async_copy(g_out, gout_any, lsem.at[6])]
    stores[0].start()
    feature_sums(1)
    mine_here = zr == zh

    @pl.when(mine_here)
    def _():
        g2r[zl] = g2[1, kt, rows_at(ze * 16, 16), :]

    g_in[...] = weight_grad(lambda p: gA[p, x], N)
    stores.append(pltpu.make_async_copy(g_in, gin_any, lsem.at[7]))
    stores[1].start()

    for n in range(NL):
        got(lambda: g2r.at[n], zsem(n), no(both(mine_here, zl == n)))
    piece = g2r[0].astype(F32)
    for n in range(1, NL):
        piece = piece + g2r[n].astype(F32)
    gp[...] = piece.astype(BF16)
    asem = w.block("gal", NX * 2)
    here = (rows_at(y * QR + ze * 16, 16), cols(x))
    for d in range(NL):
        put(lambda: (gp, gn.at[here], dev(zr * 2 + k, y, zh * NL + ls[d], kt)),
            asem(x * 2 + ze), no(owns) if d == 0 else None)

    @pl.when(owns)
    def _():
        gn[here] = gp[...]

    mine = (prow(zl), cols(y))
    for c in range(2):
        for d in range(c, NL):
            got(lambda: o2r.at[c, d], ("oz", c, d))
    piece = o2[1, prow(zl), :].astype(F32)
    for c in range(2):
        for d in range(c, NL):
            piece = piece + o2r[c, d].astype(F32)
    out[mine] = (x_ref[mine].astype(F32) + piece).astype(BF16)
    for d in range(1, NL):
        put(lambda: (out.at[mine], out.at[mine], dev(x, y, zh * NL + ls[d], k)), ("oal", d))

    mean, rstd = st_ref[:, 0:1], st_ref[:, 1:2]
    sc[...] = (x_ref[...].astype(F32) - mean) * rstd
    stb[...] = jnp.zeros((TOK, TOK), F32)
    for q in range(NX):
        for e in range(2):
            got(lambda: gn.at[rows_at(y * QR + e * 16, 16), pl.ds(q * PC, PC)], asem(q * 2 + e),
                no(both(owns, x == q, ze == e)))
    for i in (1, 0, 2):
        put(lambda: (gn.at[quarter], gn.at[quarter], dev(x, ys[i], z, k)), ("gay", i))
    gz = gn[quarter, :].astype(F32) * gain
    lane = lax.broadcasted_iota(jnp.int32, (QR, TOK), 1)
    first = jnp.sum(gz, -1, keepdims=True)
    second = jnp.sum(gz * sc[quarter, :], -1, keepdims=True)
    stb[quarter, :] = jnp.where(lane == 0, first, jnp.where(lane == 1, second, 0.0))
    stats[0] = stb[...].T[0:8, :]
    for dx in range(4):
        for dy in range(4):
            if dx or dy:
                put(lambda: (stats.at[0], stats.at[dx * 4 + dy],
                             dev(lax.rem(x + dx, NX), lax.rem(y + dy, NY), z, k)), ("ls", dx, dy))
    from_l = [lax.rem(zl + NL - d, NL) for d in range(NL)]
    for d in range(1, NL):
        got(lambda: out.at[prow(from_l[d]), cols(y)], ("oal", d))
    for i in (1, 0, 2):
        put(lambda: (out.at[:, cols(y)], out.at[:, cols(y)], dev(x, ys[i], z, k)), ("oay", i))
    for n in range(1, 16):
        got(lambda: stats.at[n], ("ls", n // 4, n % 4))
    sums_all = stats[0]
    for n in range(1, 16):
        sums_all = sums_all + stats[n]
    first, second = unpack_pair(sums_all)
    for i in range(3):
        got(lambda: gn.at[rows_at(from_y[i] * QR, QR)], ("gay", i))
    gz = gn[...].astype(F32) * gain
    delta = rstd * (gz - first / D - sc[...] * (second / D))
    gx[...] = (cot_ref[...].astype(F32) + delta).astype(BF16)
    stores.append(pltpu.make_async_copy(gx, gx_any, lsem.at[9]))
    stores[2].start()
    for i in range(3):
        got(lambda: out.at[:, cols(from_y[i])], ("oay", i))
    stores.append(pltpu.make_async_copy(out, out_any, lsem.at[8]))
    stores[3].start()
    w.finish()
    for store in stores:
        store.wait()
    assert len(w.sent) <= N_SEND and len(w.slots) <= N_RECV


def hand_kernel(a, b, c, d, ao, bo, co, do, sem):
    copies = [
        pltpu.make_async_copy(src, dst, sem.at[i])
        for i, (src, dst) in enumerate(((a, ao), (b, bo), (c, co), (d, do)))
    ]
    for copy in copies:
        copy.start()
    for copy in copies:
        copy.wait()


def per_device(inputs, cotangent, ln_gain, ln_bias, w_in, w_out):
    dma = pltpu.SemaphoreType.DMA
    tile = jax.ShapeDtypeStruct((TOK, FEAT), BF16)
    grad = jax.ShapeDtypeStruct((HIDT, FEAT), BF16)

    def vb(*shape):
        return pltpu.VMEM(shape, BF16)

    def vf(*shape):
        return pltpu.VMEM(shape, F32)

    results = pl.pallas_call(
        layer_kernel,
        name="layer",
        out_shape=[tile, tile, grad, grad],
        in_specs=[HBM] * 6,
        out_specs=[HBM] * 4,
        scratch_shapes=[
            vb(TOK, FEAT), vb(TOK, FEAT), vf(FEAT), vf(FEAT), vb(HIDT, FEAT), vb(HIDT, FEAT),
            vb(4, TOK, FEAT), vb(4, TOK, FEAT), vb(4, TOK, FEAT), vf(4, 8, TOK), vf(4, 8, TOK),
            vf(2, FEAT), vf(TOK, TOK),
            vf(4, HIDT, TOK), vf(2, HIDT, TOK), vb(2, HIDT, TOK), vb(2, HIDT, TOK),
            vb(3, HIDT, TOK), vb(3, HIDT, TOK), vb(HIDT, TOK), vb(2, HIDT, TOK),
            vb(4, HIDT, TOK), vb(2, HIDT, TOK),
            vb(NX, HIDT, PC), vb(4, NX, HIDT, TOK), vf(2, 2, TOK, PC), vb(2, 2, TOK, PC), vb(2, 3, 2, QR, PC),
            vb(2, 2, QR, PC), vb(NL, PR, PC), vb(PR, PC), vb(TOK, FEAT), vf(TOK, FEAT), vf(TOK, TOK),
            vb(2, TOK, FEAT), vb(2, TOK, FEAT), vf(2, TOK, FEAT), vb(2, TOK, FEAT),
            vb(2, 3, TOK, PC), vb(2, TOK, PC), vb(2, NL, PR, PC), vf(16, 8, TOK),
            vb(TOK, FEAT), vb(TOK, FEAT), vb(HIDT, FEAT), vb(HIDT, FEAT),
            dma((N_SEND,)), dma((N_RECV,)), dma((10,)),
        ],
        compiler_params=pltpu.CompilerParams(
            collective_id=0, has_side_effects=True, vmem_limit_bytes=63 << 20
        ),
    )(inputs, cotangent, ln_gain, ln_bias, w_in.T, w_out)
    out, gx, g_in, g_out = pl.pallas_call(
        hand_kernel,
        name="hand",
        out_shape=[tile, tile, grad, grad],
        in_specs=[VMEM] * 4,
        out_specs=[HBM] * 4,
        scratch_shapes=[dma((4,))],
    )(*results)
    return out, gx, g_in.T, g_out


def solution(mesh):
    return jax.shard_map(
        per_device,
        mesh=mesh,
        in_specs=(
            P("row", "col"),
            P("row", "col"),
            P("col"),
            P("col"),
            P("row", ("section", "col")),
            P(("section", "row"), "col"),
        ),
        out_specs=(
            P("row", "col"),
            P("row", "col"),
            P("row", ("section", "col")),
            P(("section", "row"), "col"),
        ),
        check_vma=False,
    )
```

```python
import jax
import jax.numpy as jnp
from jax import lax
from jax.experimental import pallas as pl
from jax.experimental.pallas import tpu as pltpu
from jax.sharding import PartitionSpec as P

EPS = 1e-05
SLOPE = 0.7978845608028654
CUBIC = 0.044715
F32, BF16 = jnp.float32, jnp.bfloat16
NX, NY, NZ, NL = 4, 4, 16, 8
TOK, FEAT, HIDT = 128, 1536, 192
D = NX * FEAT
QR = TOK // NY
PR, PC = TOK // NL, FEAT // NY
VMEM = pl.BlockSpec(memory_space=pltpu.VMEM)
HBM = pl.BlockSpec(memory_space=pltpu.HBM)
NT = (((1,), (1,)), ((), ()))
TN = (((0,), (0,)), ((), ()))


def gelu_both(values):
    inner = jnp.tanh(SLOPE * (values + CUBIC * values * values * values))
    act = 0.5 * values * (1.0 + inner)
    slope = 0.5 * (1.0 + inner) + 0.5 * values * (1.0 - inner * inner) * SLOPE * (
        1.0 + 3.0 * CUBIC * values * values
    )
    return act, slope


def place():
    section, row, x = lax.axis_index("section"), lax.axis_index("row"), lax.axis_index("col")
    y, zl = lax.div(section, NL), lax.rem(section, NL)
    zh, k = lax.div(row, 2), lax.rem(row, 2)
    return x, y, zh * NL + zl, zh, zl, k, row


def dev(x, y, z, k):
    return (y * NL + lax.rem(z, NL), lax.div(z, NL) * 2 + k, x)

def al(value, mult):
    return pl.multiple_of(value, mult)


def pack_pair(first, second):
    lane = lax.broadcasted_iota(jnp.int32, (TOK, TOK), 1)
    both = jnp.where(lane == 0, first, jnp.where(lane == 1, second, 0.0))
    return both.T[0:8, :]


def unpack_pair(packed):
    both = jnp.concatenate([packed, jnp.zeros((TOK - 8, TOK), F32)], axis=0).T
    return both[:, 0:1], both[:, 1:2]


def arrived(ref, sem):
    pltpu.make_async_copy(ref, ref, sem).wait()


class Wires:
    def __init__(self, ssem, rsem):
        self.ssem, self.rsem = ssem, rsem
        self.slots, self.sent = {}, []

    def slot(self, *name):
        return self.rsem.at[self.slots.setdefault(name, len(self.slots))]

    def block(self, name, size):
        base = len(self.slots)
        for i in range(size):
            self.slot(name, i)
        return lambda i: self.rsem.at[base + i]

    def put(self, make, name, pred=None):
        rsem = self.slot(*name) if isinstance(name, tuple) else name
        ssem = self.ssem.at[len(self.sent)]

        src, dst, to = make()

        def copy():
            return pltpu.make_async_remote_copy(
                src_ref=src, dst_ref=dst, send_sem=ssem, recv_sem=rsem,
                device_id=to, device_id_type=pl.DeviceIdType.MESH,
            )

        when(pred, lambda: copy().start())
        self.sent.append((pred, copy))

    def got(self, make, name, pred=None):
        ref = make()
        sem = self.slot(*name) if isinstance(name, tuple) else name
        when(pred, lambda: arrived(ref, sem))

    def finish(self):
        for pred, copy in self.sent:
            when(pred, lambda copy=copy: copy().wait_send())


def when(pred, act):
    if pred is None:
        act()
    else:
        pl.when(pred)(act)


def both(*flags):
    result = flags[0]
    for flag in flags[1:]:
        result = jnp.logical_and(result, flag)
    return result


N_SEND, N_RECV = 190, 160


def layer_kernel(
    x_any, cot_any, gain_any, bias_any, win_any, wout_any,
    out_any, gx_any, gin_any, gout_any,
    x_ref, cot_ref, gain_ref, bias_ref, w_in, w_out,
    X, C, N, sums, pairs, gb, st_ref,
    hs, hr, us, ur, qs, qr, ts, tr, aT, at,
    WX, gA, g0, gq, g1r, g2, g2r, gp, gn, sc, stb,
    os, orr, o0, o1, o1r, o2, o2r, stats, out, gx, g_in, g_out,
    ssem, rsem, dsem,
):
    x, y, z, zh, zl, k, r = place()
    no = jnp.logical_not
    w = Wires(ssem, rsem)
    put, got = w.put, w.got
    loads = [
        pltpu.make_async_copy(src, dst, dsem.at[i])
        for i, (src, dst) in enumerate((
            (x_any, x_ref), (cot_any, cot_ref), (gain_any, gain_ref),
            (bias_any, bias_ref), (win_any, w_in), (wout_any, w_out),
        ))
    ]
    for load in loads:
        load.start()
    zm, zp = NZ - 1 - z, (1 - zh) * NL + zl
    par = lax.rem(zl, 2)
    zn = z + 1 - 2 * par
    xs = [lax.rem(x + d, NX) for d in (1, 2, 3)]
    ys = [lax.rem(y + d, NY) for d in (1, 2, 3)]
    zs = [lax.rem(z + d, NZ) for d in range(1, NZ)]
    ls = [lax.rem(zl + d, NL) for d in range(NL)]
    diag = r == x
    zb, kb = lax.div(x, 2), lax.rem(x, 2)
    home = zb == zh
    beside = jnp.logical_and(home, k != kb)
    core, pair = dev(x, y, z, 1 - k), dev(x, y, zp, k)
    zr, kt, ze = lax.div(zl, 4), lax.rem(lax.div(zl, 2), 2), lax.rem(zl, 2)
    owns = both(zr == zb, kt == k, k == kb)

    barrier = pltpu.get_barrier_semaphore()

    def greet(peer, pred=None):
        when(pred, lambda: pl.semaphore_signal(
            barrier, inc=1, device_id=peer, device_id_type=pl.DeviceIdType.MESH))

    for d in (8, 7, 9, 6, 10, 5, 11, 4, 12, 3, 13, 2, 14, 1, 15):
        greet(dev(x, y, zs[d - 1], k))
    greet(core)
    greet(dev(x, y, zm, 1 - k))
    for dx in range(4):
        for dy in range(4):
            if dx or dy:
                greet(dev(lax.rem(x + dx, NX), lax.rem(y + dy, NY), z, k))
    section = lax.axis_index("section")
    for half in range(2):
        greet((section, x, half * 2 + k), no(jnp.logical_and(diag, zh == half)))
    greet(dev(r, y, z, 1 - k), no(diag))
    for q in range(NX):
        for e in range(2):
            greet(dev(q, y, zh * NL + zb * 4 + k * 2 + e, kb),
                  no(both(owns, x == q, lax.rem(zl, 2) == e)))

    def num(flag):
        return flag.astype(jnp.int32)
    total = 15 + 2 + 15 + 2 - num(diag) + 3 * num(beside) + 8 - num(owns)

    loads[0].wait()
    rows = x_ref[...].astype(F32)
    sums[0] = pack_pair(
        jnp.sum(rows, -1, keepdims=True), jnp.sum(rows * rows, -1, keepdims=True)
    )
    loads[1].wait()
    loads[2].wait()
    loads[3].wait()
    pl.semaphore_wait(barrier, total)

    def rows_at(start, size):
        return pl.ds(al(start, 16), size)

    def cols(p):
        return pl.ds(al(p * PC, PC), PC)

    def prow(p):
        return pl.ds(al(p * PR, PR), PR)

    mine8 = rows_at(y * QR + par * 16, 16)
    theirs8 = rows_at(y * QR + (1 - par) * 16, 16)
    quarter = rows_at(y * QR, QR)
    front, back = (slice(None), pl.ds(0, PC)), (quarter, pl.ds(PC, FEAT - PC))
    tiles = [zh * 2 + k, zh * 2 + 1 - k, (1 - zh) * 2 + k, (1 - zh) * 2 + 1 - k]

    def spread_x(ref, name):
        for i in (1, 0, 2):
            put(lambda: (ref, ref, dev(xs[i], y, z, k)), name, diag)

    def along_y(ref, name):
        for i in (1, 0, 2):
            put(lambda: (ref, ref, dev(x, ys[i], z, k)), name + (i,))

    from_y = [lax.rem(y + NY - 1 - i, NY) for i in range(3)]
    from_x = [lax.rem(x + NX - 1 - i, NX) for i in range(3)]
    away = no(home)

    for i, p in enumerate(xs):
        put(lambda: (sums.at[0], sums.at[1 + i], dev(p, y, z, k)), ("stat", i))
    for j in range(2):
        put(lambda: (x_ref.at[mine8], X.at[r, mine8], dev(x, y, zm, k if j == 0 else 1 - k)),
            ("xz", j), jnp.logical_and(away, (k == kb) if j == 0 else (k != kb)))
    put(lambda: (x_ref.at[back], X.at[(r, *back)], core), ("xb", 1), beside)
    put(lambda: (x_ref.at[front], X.at[(r, *front)], core), ("xf", 1), beside)
    put(lambda: (cot_ref, C.at[r], core), ("cc",))

    @pl.when(diag)
    def _():
        X[(r, *back)] = x_ref[back]
        X[(r, *front)] = x_ref[front]

    for d in range(2):
        ref = X.at[(tiles[d], *back)]
        if d:
            got(lambda: ref, ("xb", d), diag)
        spread_x(ref, ("xb", d))
    gain = gain_ref[...].reshape(1, FEAT)
    bias = bias_ref[...].reshape(1, FEAT)

    @pl.when(diag)
    def _():
        gb[0:1, :] = gain
        gb[1:2, :] = bias

    spread_x(gb, ("gb",))
    spread_x(X.at[(tiles[0], *front)], ("xf", 0))
    got(lambda: X.at[(tiles[1], *front)], ("xf", 1), diag)
    spread_x(X.at[(tiles[1], *front)], ("xf", 1))
    C[r] = cot_ref[...]
    for i in range(3):
        got(lambda: sums.at[1 + i], ("stat", i))
    pairs[0] = (sums[0] + sums[1]) + (sums[2] + sums[3])
    for d, to in ((2, dev(x, y, zm, k)), (3, dev(x, y, zm, 1 - k)), (1, core)):
        put(lambda: (pairs.at[0], pairs.at[d], to), ("pair", d))
    put(lambda: (cot_ref.at[mine8], C.at[r, mine8], dev(x, y, zm, k)), ("cz",))

    def moments(d):
        first, second = unpack_pair(pairs[d])
        mean = first / D
        return mean, lax.rsqrt(second / D - mean * mean + EPS)

    mean, rstd = moments(0)
    lane = lax.broadcasted_iota(jnp.int32, (TOK, TOK), 1)
    st_ref[...] = jnp.where(lane == 0, mean, rstd)
    for d in range(2):
        ref = X.at[(tiles[d], *back)]
        got(lambda: ref, ("xb", d), no(diag))
        along_y(ref, ("yb", d))
    two, three = X.at[tiles[2], theirs8], X.at[tiles[3], theirs8]
    got(lambda: two, ("xz", 0), diag)
    put(lambda: (two, two, dev(x, y, zn, k)), ("xn",), diag)
    got(lambda: three, ("xz", 1), diag)
    spread_x(three, ("xe",))
    got(lambda: X.at[tiles[2], mine8], ("xn",), diag)
    spread_x(X.at[tiles[2], quarter], ("xq",))
    got(lambda: C.at[tiles[2], theirs8], ("cz",))
    other = C.at[tiles[2], theirs8]
    along_y(other, ("cy",))
    put(lambda: (other, other, dev(x, y, zn, k)), ("ce", 3))
    got(lambda: three, ("xe",), no(diag))
    along_y(three, ("ye",))
    put(lambda: (three, three, dev(x, y, zn, k)), ("ze", 3))
    got(lambda: X.at[tiles[2], quarter], ("xq",), no(diag))
    along_y(X.at[tiles[2], quarter], ("yq",))
    loads[4].wait()
    for i in (1, 0, 2):
        put(lambda: (w_in.at[:, cols(xs[i])], WX.at[x], dev(xs[i], y, z, k)), ("wx", i))
    WX[x] = w_in[:, cols(x)]
    got(lambda: gb, ("gb",), no(diag))

    def normalize(d):
        if d:
            got(lambda: pairs.at[d], ("pair", d))
        mean, rstd = moments(d)
        N[tiles[d]] = (
            (X[tiles[d]].astype(F32) - mean) * rstd * gb[0:1, :] + gb[1:2, :]
        ).astype(BF16)

    loads[5].wait()
    for d in range(2):
        got(lambda: X.at[(tiles[d], *front)], ("xf", d), no(diag))
        for i in range(3):
            got(lambda: X.at[tiles[d], rows_at(from_y[i] * QR, QR), pl.ds(PC, FEAT - PC)], ("yb", d, i))
        normalize(d)

    def pass_eighths(tile, arrive, leave):
        for i in range(3):
            ref = tile.at[rows_at(from_y[i] * QR + (1 - par) * 16, 16)]
            got(lambda: ref, (arrive, i))
            put(lambda: (ref, ref, dev(x, y, zn, k)), (leave, i))

    def take_eighths(tile, arrive):
        got(lambda: tile.at[mine8], (arrive, 3))
        for i in range(3):
            got(lambda: tile.at[rows_at(from_y[i] * QR + par * 16, 16)], (arrive, i))

    def hid(t):
        return lax.dot_general(w_in[...], N[t], NT, preferred_element_type=F32)

    def grad(t):
        return lax.dot_general(w_out[...], C[t], NT, preferred_element_type=F32)

    hs[0] = hid(tiles[1])
    put(lambda: (hs.at[0], hr.at[0], core), ("hc", 0))
    near = hid(tiles[0])
    pass_eighths(C.at[tiles[2]], "cy", "ce")
    pass_eighths(X.at[tiles[3]], "ye", "ze")
    got(lambda: hr.at[0], ("hc", 0))
    h_near = near + hr[0]
    us[0] = h_near.astype(BF16)
    put(lambda: (us.at[0], ur.at[1], pair), ("hz", 0))
    hs[2] = h_near
    take_eighths(C.at[tiles[2]], "ce")
    put(lambda: (C.at[tiles[2]], C.at[tiles[2]], core), ("cf",))
    got(lambda: C.at[tiles[1]], ("cc",))
    got(lambda: C.at[tiles[3]], ("cf",))
    for i in (1, 0, 2):
        qs[i] = grad(xs[i]).astype(BF16)
        put(lambda: (qs.at[i], qr.at[i], dev(xs[i], y, z, k)), ("ga", i))
    own = grad(x)
    for i in range(3):
        got(lambda: X.at[tiles[2], rows_at(from_y[i] * QR, QR)], ("yq", i))
    normalize(2)
    far = hid(tiles[2])
    take_eighths(X.at[tiles[3]], "ze")
    normalize(3)
    hs[1] = hid(tiles[3])
    put(lambda: (hs.at[1], hr.at[1], core), ("hc", 1))
    for i in range(3):
        got(lambda: qr.at[i], ("ga", i))
    ts[...] = (own + qr[0].astype(F32) + qr[1].astype(F32) + qr[2].astype(F32)).astype(BF16)
    for half in range(2):
        selfish = jnp.logical_and(diag, zh == half)
        for side in range(2):
            put(lambda: (ts, tr.at[side], (section, half * 2 + kb, r)), ("gt", side),
                jnp.logical_and(no(selfish), zb == side))

    @pl.when(diag)
    def _():
        tr[zh] = ts[...]

    got(lambda: hr.at[1], ("hc", 1))
    h_far = far + hr[1]
    us[1] = h_far.astype(BF16)
    put(lambda: (us.at[1], ur.at[0], pair), ("hz", 1))
    hs[3] = h_far
    for side in range(2):
        got(lambda: tr.at[side], ("gt", side), no(jnp.logical_and(diag, zh == side)))

    def activate(step, half):
        act, slope = gelu_both(hs[2 + step] + ur[step].astype(F32))
        gA[k * 2 + half, x] = (tr[half].astype(F32) * slope).astype(BF16)
        at[half] = act.astype(BF16)

    def spread(step, half):
        for i, p in enumerate(xs):
            put(lambda: (at.at[half], aT.at[k * 2 + half], dev(p, y, z, k)), ("ax", 0, step), diag)
        for i, p in enumerate(xs):
            put(lambda: (at.at[half], aT.at[k * 2 + half], dev(p, y, z, 1 - k)),
                ("ax", 1, step), beside)
        put(lambda: (at.at[half], aT.at[k * 2 + half], core), ("ax", 1, step), beside)

        @pl.when(diag)
        def _():
            aT[k * 2 + half] = at[half]

        ref = gA.at[k * 2 + half, x]
        for i in (1, 0, 2):
            put(lambda: (ref, ref, dev(xs[i], y, z, k)), ("gg", step, i))
        put(lambda: (ref, ref, core), ("gc", step))

    def part_o(pos):
        return lax.dot_general(aT[pos], w_out[...], TN, preferred_element_type=F32)

    halves = (1 - zh, zh)

    def outputs(c):
        step, half = 1 - c, halves[c]
        held, unheld = k * 2 + half, (1 - k) * 2 + half
        got(lambda: aT.at[held], ("ax", 0, step), no(diag))
        got(lambda: aT.at[unheld], ("ax", 1, step))
        os[c] = part_o(unheld).astype(BF16)
        put(lambda: (os.at[c], orr.at[c], core), ("oc", c))
        o0[c] = part_o(held)
        for i in (0, 2, 1):
            ref = gA.at[held, from_x[i]]
            got(lambda: ref, ("gg", step, i))
            put(lambda: (ref, ref, core), ("gf", step, i))
        got(lambda: orr.at[c], ("oc", c))
        o1[c] = (o0[c] + orr[c].astype(F32)).astype(BF16)
        for i in (1, 0, 2):
            put(lambda: (o1.at[c, :, cols(ys[i])], o1r.at[c, i], dev(x, ys[i], z, k)), ("oy", c, i))
    def features(c):
        step, half = 1 - c, halves[c]
        unheld = (1 - k) * 2 + half
        if c == 0:
            for i in range(3):
                got(lambda: WX.at[from_x[i]], ("wx", i))
        got(lambda: gA.at[unheld, x], ("gc", step))
        for i in (0, 2, 1):
            got(lambda: gA.at[unheld, from_x[i]], ("gf", step, i))
        slab = WX[...].reshape(NX * HIDT, PC)
        for j in range(2):
            g0[c, j] = lax.dot_general(
                gA[j * 2 + half].reshape(NX * HIDT, TOK), slab, TN, preferred_element_type=F32)
        gq[c] = g0[c].astype(BF16)
        for i in (1, 0, 2):
            put(lambda: (gq.at[c, :, rows_at(ys[i] * QR, QR)], g1r.at[c, i],
                         dev(x, ys[i], z, k)), ("gy", c, i))

    zsem = w.block("gz", NL)

    def sums_y(c):
        for i in range(3):
            got(lambda: o1r.at[c, i], ("oy", c, i))
        o2[c] = (
            o1[c, :, cols(y)].astype(F32) + o1r[c, 0].astype(F32)
            + o1r[c, 1].astype(F32) + o1r[c, 2].astype(F32)
        ).astype(BF16)
        for d in range(c, NL):
            target = halves[c] * NL + ls[d]
            put(lambda: (o2.at[c, prow(ls[d])], o2r.at[c, d], dev(x, y, target, k)), ("oz", c, d))

    def feature_sums(c):
        for i in range(3):
            got(lambda: g1r.at[c, i], ("gy", c, i))
        g2[c] = (
            g0[c, :, quarter, :] + g1r[c, 0].astype(F32)
            + g1r[c, 1].astype(F32) + g1r[c, 2].astype(F32)
        ).astype(BF16)
        for j in range(2):
            for e in range(2):
                target = halves[c] * NL + zh * 4 + j * 2 + e
                put(lambda: (g2.at[c, j, pl.ds(e * 16, 16)], g2r.at[zl], dev(x, y, target, k)),
                    zsem(zl), (z != target) if c else None)

    got(lambda: ur.at[1], ("hz", 0))
    activate(1, 1 - zh)
    spread(1, 1 - zh)
    got(lambda: ur.at[0], ("hz", 1))
    activate(0, zh)
    spread(0, zh)
    outputs(0)
    outputs(1)
    features(0)
    features(1)
    sums_y(0)
    sums_y(1)
    feature_sums(0)

    def weight_grad(left, right):
        wide = jnp.concatenate([left((t % 2) * 2 + t // 2) for t in range(4)], axis=1)
        tall = right[...].reshape(4 * TOK, FEAT)
        return jnp.dot(wide, tall, preferred_element_type=F32).astype(BF16)

    g_out[...] = weight_grad(lambda p: aT[p], C)
    stores = [pltpu.make_async_copy(g_out, gout_any, dsem.at[6])]
    stores[0].start()
    feature_sums(1)
    mine_here = zr == zh

    @pl.when(mine_here)
    def _():
        g2r[zl] = g2[1, kt, rows_at(ze * 16, 16), :]

    g_in[...] = weight_grad(lambda p: gA[p, x], N)
    stores.append(pltpu.make_async_copy(g_in, gin_any, dsem.at[7]))
    stores[1].start()

    for n in range(NL):
        got(lambda: g2r.at[n], zsem(n), no(both(mine_here, zl == n)))
    piece = g2r[0].astype(F32)
    for n in range(1, NL):
        piece = piece + g2r[n].astype(F32)
    gp[...] = piece.astype(BF16)
    asem = w.block("gal", NX * 2)
    here = (rows_at(y * QR + ze * 16, 16), cols(x))
    for d in range(NL):
        put(lambda: (gp, gn.at[here], dev(zr * 2 + k, y, zh * NL + ls[d], kt)),
            asem(x * 2 + ze), no(owns) if d == 0 else None)

    @pl.when(owns)
    def _():
        gn[here] = gp[...]

    mine = (prow(zl), cols(y))
    for c in range(2):
        for d in range(c, NL):
            got(lambda: o2r.at[c, d], ("oz", c, d))
    piece = o2[1, prow(zl), :].astype(F32)
    for c in range(2):
        for d in range(c, NL):
            piece = piece + o2r[c, d].astype(F32)
    out[mine] = (x_ref[mine].astype(F32) + piece).astype(BF16)
    lsem = w.block("oal", NL)
    for d in (4, 3, 5, 2, 6, 1, 7):
        put(lambda: (out.at[mine], out.at[mine], dev(x, y, zh * NL + ls[d], k)), lsem(zl))

    mean, rstd = st_ref[:, 0:1], st_ref[:, 1:2]
    sc[...] = (x_ref[...].astype(F32) - mean) * rstd
    stb[...] = jnp.zeros((TOK, TOK), F32)
    group = lax.div(zl, 4)
    groups = (group, 1 - group)

    def strip(n, q):
        return out.at[(rows_at(groups[n] * 64, 64), cols(q))]

    def send_strip(n):
        for i in range(4):
            source = groups[n] * 4 + i
            got(lambda: out.at[prow(source), cols(y)], lsem(source),
                (zl != source) if n == 0 else None)
        for i in (1, 0, 2):
            put(lambda: (strip(n, y), strip(n, y), dev(x, ys[i], z, k)), ("oay", n, i))

    send_strip(0)
    for q in range(NX):
        for e in range(2):
            got(lambda: gn.at[rows_at(y * QR + e * 16, 16), pl.ds(q * PC, PC)], asem(q * 2 + e),
                no(both(owns, x == q, ze == e)))
    for i in (1, 0, 2):
        put(lambda: (gn.at[quarter], gn.at[quarter], dev(x, ys[i], z, k)), ("gay", i))
    gz = gn[quarter, :].astype(F32) * gain
    lane = lax.broadcasted_iota(jnp.int32, (QR, TOK), 1)
    first = jnp.sum(gz, -1, keepdims=True)
    second = jnp.sum(gz * sc[quarter, :], -1, keepdims=True)
    stb[quarter, :] = jnp.where(lane == 0, first, jnp.where(lane == 1, second, 0.0))
    stats[0] = stb[...].T[0:8, :]
    for dx in range(4):
        for dy in range(4):
            if dx or dy:
                put(lambda: (stats.at[0], stats.at[dx * 4 + dy],
                             dev(lax.rem(x + dx, NX), lax.rem(y + dy, NY), z, k)), ("ls", dx, dy))
    send_strip(1)
    for n in range(1, 16):
        got(lambda: stats.at[n], ("ls", n // 4, n % 4))
    sums_all = stats[0]
    for n in range(1, 16):
        sums_all = sums_all + stats[n]
    first, second = unpack_pair(sums_all)
    for i in range(3):
        got(lambda: gn.at[rows_at(from_y[i] * QR, QR)], ("gay", i))
    gz = gn[...].astype(F32) * gain
    delta = rstd * (gz - first / D - sc[...] * (second / D))
    gx[...] = (cot_ref[...].astype(F32) + delta).astype(BF16)
    stores.append(pltpu.make_async_copy(gx, gx_any, dsem.at[9]))
    stores[2].start()
    for n in range(2):
        for i in range(3):
            got(lambda: strip(n, from_y[i]), ("oay", n, i))
    stores.append(pltpu.make_async_copy(out, out_any, dsem.at[8]))
    stores[3].start()
    w.finish()
    for store in stores:
        store.wait()
    assert len(w.sent) <= N_SEND and len(w.slots) <= N_RECV


def hand_kernel(a, b, c, d, ao, bo, co, do, sem):
    copies = [
        pltpu.make_async_copy(src, dst, sem.at[i])
        for i, (src, dst) in enumerate(((a, ao), (b, bo), (c, co), (d, do)))
    ]
    for copy in copies:
        copy.start()
    for copy in copies:
        copy.wait()


def per_device(inputs, cotangent, ln_gain, ln_bias, w_in, w_out):
    dma = pltpu.SemaphoreType.DMA
    tile = jax.ShapeDtypeStruct((TOK, FEAT), BF16)
    grad = jax.ShapeDtypeStruct((HIDT, FEAT), BF16)

    def vb(*shape):
        return pltpu.VMEM(shape, BF16)

    def vf(*shape):
        return pltpu.VMEM(shape, F32)

    results = pl.pallas_call(
        layer_kernel,
        name="layer",
        out_shape=[tile, tile, grad, grad],
        in_specs=[HBM] * 6,
        out_specs=[HBM] * 4,
        scratch_shapes=[
            vb(TOK, FEAT), vb(TOK, FEAT), vf(FEAT), vf(FEAT), vb(HIDT, FEAT), vb(HIDT, FEAT),
            vb(4, TOK, FEAT), vb(4, TOK, FEAT), vb(4, TOK, FEAT), vf(4, 8, TOK), vf(4, 8, TOK),
            vf(2, FEAT), vf(TOK, TOK),
            vf(4, HIDT, TOK), vf(2, HIDT, TOK), vb(2, HIDT, TOK), vb(2, HIDT, TOK),
            vb(3, HIDT, TOK), vb(3, HIDT, TOK), vb(HIDT, TOK), vb(2, HIDT, TOK),
            vb(4, HIDT, TOK), vb(2, HIDT, TOK),
            vb(NX, HIDT, PC), vb(4, NX, HIDT, TOK), vf(2, 2, TOK, PC), vb(2, 2, TOK, PC), vb(2, 3, 2, QR, PC),
            vb(2, 2, QR, PC), vb(NL, PR, PC), vb(PR, PC), vb(TOK, FEAT), vf(TOK, FEAT), vf(TOK, TOK),
            vb(2, TOK, FEAT), vb(2, TOK, FEAT), vf(2, TOK, FEAT), vb(2, TOK, FEAT),
            vb(2, 3, TOK, PC), vb(2, TOK, PC), vb(2, NL, PR, PC), vf(16, 8, TOK),
            vb(TOK, FEAT), vb(TOK, FEAT), vb(HIDT, FEAT), vb(HIDT, FEAT),
            dma((N_SEND,)), dma((N_RECV,)), dma((10,)),
        ],
        compiler_params=pltpu.CompilerParams(
            collective_id=0, has_side_effects=True, vmem_limit_bytes=63 << 20
        ),
    )(inputs, cotangent, ln_gain, ln_bias, w_in.T, w_out)
    out, gx, g_in, g_out = pl.pallas_call(
        hand_kernel,
        name="hand",
        out_shape=[tile, tile, grad, grad],
        in_specs=[VMEM] * 4,
        out_specs=[HBM] * 4,
        scratch_shapes=[dma((4,))],
    )(*results)
    return out, gx, g_in.T, g_out


def solution(mesh):
    return jax.shard_map(
        per_device,
        mesh=mesh,
        in_specs=(
            P("row", "col"),
            P("row", "col"),
            P("col"),
            P("col"),
            P("row", ("section", "col")),
            P(("section", "row"), "col"),
        ),
        out_specs=(
            P("row", "col"),
            P("row", "col"),
            P("row", ("section", "col")),
            P(("section", "row"), "col"),
        ),
        check_vma=False,
    )
```

```python
import jax
import jax.numpy as jnp
from jax import lax
from jax.experimental import pallas as pl
from jax.experimental.pallas import tpu as pltpu
from jax.sharding import PartitionSpec as P

EPS = 1e-05
SLOPE = 0.7978845608028654
CUBIC = 0.044715
F32, BF16 = jnp.float32, jnp.bfloat16
NX, NY, NZ, NL = 4, 4, 16, 8
TOK, FEAT, HIDT = 128, 1536, 192
D = NX * FEAT
QR = TOK // NY
PR, PC = TOK // NL, FEAT // NY
VMEM = pl.BlockSpec(memory_space=pltpu.VMEM)
HBM = pl.BlockSpec(memory_space=pltpu.HBM)
NT = (((1,), (1,)), ((), ()))
TN = (((0,), (0,)), ((), ()))


def gelu_both(values):
    inner = jnp.tanh(SLOPE * (values + CUBIC * values * values * values))
    act = 0.5 * values * (1.0 + inner)
    slope = 0.5 * (1.0 + inner) + 0.5 * values * (1.0 - inner * inner) * SLOPE * (
        1.0 + 3.0 * CUBIC * values * values
    )
    return act, slope


def place():
    section, row, x = lax.axis_index("section"), lax.axis_index("row"), lax.axis_index("col")
    y, zl = lax.div(section, NL), lax.rem(section, NL)
    zh, k = lax.div(row, 2), lax.rem(row, 2)
    return x, y, zh * NL + zl, zh, zl, k, row


def dev(x, y, z, k):
    return (y * NL + lax.rem(z, NL), lax.div(z, NL) * 2 + k, x)

def al(value, mult):
    return pl.multiple_of(value, mult)


def pack_pair(first, second):
    lane = lax.broadcasted_iota(jnp.int32, (TOK, TOK), 1)
    both = jnp.where(lane == 0, first, jnp.where(lane == 1, second, 0.0))
    return both.T[0:8, :]


def unpack_pair(packed):
    both = jnp.concatenate([packed, jnp.zeros((TOK - 8, TOK), F32)], axis=0).T
    return both[:, 0:1], both[:, 1:2]


def arrived(ref, sem):
    pltpu.make_async_copy(ref, ref, sem).wait()


class Wires:
    def __init__(self, ssem, rsem):
        self.ssem, self.rsem = ssem, rsem
        self.slots, self.sent = {}, []

    def slot(self, *name):
        return self.rsem.at[self.slots.setdefault(name, len(self.slots))]

    def block(self, name, size):
        base = len(self.slots)
        for i in range(size):
            self.slot(name, i)
        return lambda i: self.rsem.at[base + i]

    def put(self, make, name, pred=None):
        rsem = self.slot(*name) if isinstance(name, tuple) else name
        ssem = self.ssem.at[len(self.sent)]

        src, dst, to = make()

        def copy():
            return pltpu.make_async_remote_copy(
                src_ref=src, dst_ref=dst, send_sem=ssem, recv_sem=rsem,
                device_id=to, device_id_type=pl.DeviceIdType.MESH,
            )

        when(pred, lambda: copy().start())
        self.sent.append((pred, copy))

    def got(self, make, name, pred=None):
        ref = make()
        sem = self.slot(*name) if isinstance(name, tuple) else name
        when(pred, lambda: arrived(ref, sem))

    def finish(self):
        for pred, copy in self.sent:
            when(pred, lambda copy=copy: copy().wait_send())


def when(pred, act):
    if pred is None:
        act()
    else:
        pl.when(pred)(act)


def both(*flags):
    result = flags[0]
    for flag in flags[1:]:
        result = jnp.logical_and(result, flag)
    return result


N_SEND, N_RECV = 190, 160


def layer_kernel(
    x_any, cot_any, gain_any, bias_any, win_any, wout_any,
    out_any, gx_any, gin_any, gout_any,
    x_ref, cot_ref, gain_ref, bias_ref, w_in, w_out,
    X, C, N, sums, pairs, gb, st_ref,
    hs, hr, us, ur, qs, qr, ts, tr, aT, at,
    WX, gA, g0, gq, g1r, g2, g2r, gp, gn, sc, stb,
    os, orr, o0, o1, o1r, o2, o2r, stats, out, gx, g_in, g_out,
    ssem, rsem, dsem,
):
    x, y, z, zh, zl, k, r = place()
    no = jnp.logical_not
    w = Wires(ssem, rsem)
    put, got = w.put, w.got
    loads = [
        pltpu.make_async_copy(src, dst, dsem.at[i])
        for i, (src, dst) in enumerate((
            (x_any, x_ref), (cot_any, cot_ref), (gain_any, gain_ref),
            (bias_any, bias_ref), (win_any, w_in), (wout_any, w_out),
        ))
    ]
    for load in loads:
        load.start()
    zm, zp = NZ - 1 - z, (1 - zh) * NL + zl
    par = lax.rem(zl, 2)
    zn = z + 1 - 2 * par
    xs = [lax.rem(x + d, NX) for d in (1, 2, 3)]
    ys = [lax.rem(y + d, NY) for d in (1, 2, 3)]
    zs = [lax.rem(z + d, NZ) for d in range(1, NZ)]
    ls = [lax.rem(zl + d, NL) for d in range(NL)]
    diag = r == x
    zb, kb = lax.div(x, 2), lax.rem(x, 2)
    home = zb == zh
    beside = jnp.logical_and(home, k != kb)
    core, pair = dev(x, y, z, 1 - k), dev(x, y, zp, k)
    zr, kt, ze = lax.div(zl, 4), lax.rem(lax.div(zl, 2), 2), lax.rem(zl, 2)
    owns = both(zr == zb, kt == k, k == kb)

    barrier = pltpu.get_barrier_semaphore()

    def greet(peer, pred=None):
        when(pred, lambda: pl.semaphore_signal(
            barrier, inc=1, device_id=peer, device_id_type=pl.DeviceIdType.MESH))

    for d in (8, 7, 9, 6, 10, 5, 11, 4, 12, 3, 13, 2, 14, 1, 15):
        greet(dev(x, y, zs[d - 1], k))
    greet(core)
    greet(dev(x, y, zm, 1 - k))
    for dx in range(4):
        for dy in range(4):
            if dx or dy:
                greet(dev(lax.rem(x + dx, NX), lax.rem(y + dy, NY), z, k))
    section = lax.axis_index("section")
    for half in range(2):
        greet((section, x, half * 2 + k), no(jnp.logical_and(diag, zh == half)))
    greet(dev(r, y, z, 1 - k), no(diag))
    for q in range(NX):
        for e in range(2):
            greet(dev(q, y, zh * NL + zb * 4 + k * 2 + e, kb),
                  no(both(owns, x == q, lax.rem(zl, 2) == e)))

    def num(flag):
        return flag.astype(jnp.int32)
    total = 15 + 2 + 15 + 2 - num(diag) + 3 * num(beside) + 8 - num(owns)

    loads[0].wait()
    rows = x_ref[...].astype(F32)
    sums[0] = pack_pair(
        jnp.sum(rows, -1, keepdims=True), jnp.sum(rows * rows, -1, keepdims=True)
    )
    loads[1].wait()
    loads[2].wait()
    loads[3].wait()
    pl.semaphore_wait(barrier, total)

    def rows_at(start, size):
        return pl.ds(al(start, 16), size)

    def cols(p):
        return pl.ds(al(p * PC, PC), PC)

    def prow(p):
        return pl.ds(al(p * PR, PR), PR)

    mine8 = rows_at(y * QR + par * 16, 16)
    theirs8 = rows_at(y * QR + (1 - par) * 16, 16)
    quarter = rows_at(y * QR, QR)
    front, back = (slice(None), pl.ds(0, PC)), (quarter, pl.ds(PC, FEAT - PC))
    tiles = [zh * 2 + k, zh * 2 + 1 - k, (1 - zh) * 2 + k, (1 - zh) * 2 + 1 - k]

    def spread_x(ref, name):
        for i in (1, 0, 2):
            put(lambda: (ref, ref, dev(xs[i], y, z, k)), name, diag)

    def along_y(ref, name):
        for i in (1, 0, 2):
            put(lambda: (ref, ref, dev(x, ys[i], z, k)), name + (i,))

    from_y = [lax.rem(y + NY - 1 - i, NY) for i in range(3)]
    from_x = [lax.rem(x + NX - 1 - i, NX) for i in range(3)]
    away = no(home)

    for i, p in enumerate(xs):
        put(lambda: (sums.at[0], sums.at[1 + i], dev(p, y, z, k)), ("stat", i))
    for j in range(2):
        put(lambda: (x_ref.at[mine8], X.at[r, mine8], dev(x, y, zm, k if j == 0 else 1 - k)),
            ("xz", j), jnp.logical_and(away, (k == kb) if j == 0 else (k != kb)))
    put(lambda: (x_ref.at[back], X.at[(r, *back)], core), ("xb", 1), beside)
    put(lambda: (x_ref.at[front], X.at[(r, *front)], core), ("xf", 1), beside)
    put(lambda: (cot_ref, C.at[r], core), ("cc",))

    @pl.when(diag)
    def _():
        X[(r, *back)] = x_ref[back]
        X[(r, *front)] = x_ref[front]

    for d in range(2):
        ref = X.at[(tiles[d], *back)]
        if d:
            got(lambda: ref, ("xb", d), diag)
        spread_x(ref, ("xb", d))
    gain = gain_ref[...].reshape(1, FEAT)
    bias = bias_ref[...].reshape(1, FEAT)

    @pl.when(diag)
    def _():
        gb[0:1, :] = gain
        gb[1:2, :] = bias

    spread_x(gb, ("gb",))
    spread_x(X.at[(tiles[0], *front)], ("xf", 0))
    got(lambda: X.at[(tiles[1], *front)], ("xf", 1), diag)
    spread_x(X.at[(tiles[1], *front)], ("xf", 1))
    C[r] = cot_ref[...]
    for i in range(3):
        got(lambda: sums.at[1 + i], ("stat", i))
    pairs[0] = (sums[0] + sums[1]) + (sums[2] + sums[3])
    for d, to in ((2, dev(x, y, zm, k)), (3, dev(x, y, zm, 1 - k)), (1, core)):
        put(lambda: (pairs.at[0], pairs.at[d], to), ("pair", d))
    put(lambda: (cot_ref.at[mine8], C.at[r, mine8], dev(x, y, zm, k)), ("cz",))

    def moments(d):
        first, second = unpack_pair(pairs[d])
        mean = first / D
        return mean, lax.rsqrt(second / D - mean * mean + EPS)

    mean, rstd = moments(0)
    lane = lax.broadcasted_iota(jnp.int32, (TOK, TOK), 1)
    st_ref[...] = jnp.where(lane == 0, mean, rstd)
    for d in range(2):
        ref = X.at[(tiles[d], *back)]
        got(lambda: ref, ("xb", d), no(diag))
        along_y(ref, ("yb", d))
    two, three = X.at[tiles[2], theirs8], X.at[tiles[3], theirs8]
    got(lambda: two, ("xz", 0), diag)
    put(lambda: (two, two, dev(x, y, zn, k)), ("xn",), diag)
    got(lambda: three, ("xz", 1), diag)
    spread_x(three, ("xe",))
    got(lambda: X.at[tiles[2], mine8], ("xn",), diag)
    spread_x(X.at[tiles[2], quarter], ("xq",))
    got(lambda: C.at[tiles[2], theirs8], ("cz",))
    other = C.at[tiles[2], theirs8]
    along_y(other, ("cy",))
    put(lambda: (other, other, dev(x, y, zn, k)), ("ce", 3))
    got(lambda: three, ("xe",), no(diag))
    along_y(three, ("ye",))
    put(lambda: (three, three, dev(x, y, zn, k)), ("ze", 3))
    got(lambda: X.at[tiles[2], quarter], ("xq",), no(diag))
    along_y(X.at[tiles[2], quarter], ("yq",))
    loads[4].wait()
    got(lambda: gb, ("gb",), no(diag))

    def normalize(d):
        if d:
            got(lambda: pairs.at[d], ("pair", d))
        mean, rstd = moments(d)
        N[tiles[d]] = (
            (X[tiles[d]].astype(F32) - mean) * rstd * gb[0:1, :] + gb[1:2, :]
        ).astype(BF16)

    loads[5].wait()
    for d in range(2):
        got(lambda: X.at[(tiles[d], *front)], ("xf", d), no(diag))
        for i in range(3):
            got(lambda: X.at[tiles[d], rows_at(from_y[i] * QR, QR), pl.ds(PC, FEAT - PC)], ("yb", d, i))
        normalize(d)

    def pass_eighths(tile, arrive, leave):
        for i in range(3):
            ref = tile.at[rows_at(from_y[i] * QR + (1 - par) * 16, 16)]
            got(lambda: ref, (arrive, i))
            put(lambda: (ref, ref, dev(x, y, zn, k)), (leave, i))

    def take_eighths(tile, arrive):
        got(lambda: tile.at[mine8], (arrive, 3))
        for i in range(3):
            got(lambda: tile.at[rows_at(from_y[i] * QR + par * 16, 16)], (arrive, i))

    def hid(t):
        return lax.dot_general(w_in[...], N[t], NT, preferred_element_type=F32)

    def grad(t):
        return lax.dot_general(w_out[...], C[t], NT, preferred_element_type=F32)

    hs[0] = hid(tiles[1])
    put(lambda: (hs.at[0], hr.at[0], core), ("hc", 0))
    near = hid(tiles[0])
    pass_eighths(C.at[tiles[2]], "cy", "ce")
    pass_eighths(X.at[tiles[3]], "ye", "ze")
    got(lambda: hr.at[0], ("hc", 0))
    h_near = near + hr[0]
    us[0] = h_near.astype(BF16)
    put(lambda: (us.at[0], ur.at[1], pair), ("hz", 0))
    hs[2] = h_near
    take_eighths(C.at[tiles[2]], "ce")
    put(lambda: (C.at[tiles[2]], C.at[tiles[2]], core), ("cf",))
    got(lambda: C.at[tiles[1]], ("cc",))
    got(lambda: C.at[tiles[3]], ("cf",))
    for i in (1, 0, 2):
        qs[i] = grad(xs[i]).astype(BF16)
        put(lambda: (qs.at[i], qr.at[i], dev(xs[i], y, z, k)), ("ga", i))
    own = grad(x)
    for i in (1, 0, 2):
        put(lambda: (w_in.at[:, cols(xs[i])], WX.at[x], dev(xs[i], y, z, k)), ("wx", i))
    WX[x] = w_in[:, cols(x)]
    for i in range(3):
        got(lambda: X.at[tiles[2], rows_at(from_y[i] * QR, QR)], ("yq", i))
    normalize(2)
    far = hid(tiles[2])
    take_eighths(X.at[tiles[3]], "ze")
    normalize(3)
    hs[1] = hid(tiles[3])
    put(lambda: (hs.at[1], hr.at[1], core), ("hc", 1))
    for i in range(3):
        got(lambda: qr.at[i], ("ga", i))
    ts[...] = (own + qr[0].astype(F32) + qr[1].astype(F32) + qr[2].astype(F32)).astype(BF16)
    for half in range(2):
        selfish = jnp.logical_and(diag, zh == half)
        for side in range(2):
            put(lambda: (ts, tr.at[side], (section, half * 2 + kb, r)), ("gt", side),
                jnp.logical_and(no(selfish), zb == side))

    @pl.when(diag)
    def _():
        tr[zh] = ts[...]

    got(lambda: hr.at[1], ("hc", 1))
    h_far = far + hr[1]
    us[1] = h_far.astype(BF16)
    put(lambda: (us.at[1], ur.at[0], pair), ("hz", 1))
    hs[3] = h_far
    for side in range(2):
        got(lambda: tr.at[side], ("gt", side), no(jnp.logical_and(diag, zh == side)))

    def activate(step, half):
        act, slope = gelu_both(hs[2 + step] + ur[step].astype(F32))
        gA[k * 2 + half, x] = (tr[half].astype(F32) * slope).astype(BF16)
        at[half] = act.astype(BF16)

    def spread(step, half):
        for i, p in enumerate(xs):
            put(lambda: (at.at[half], aT.at[k * 2 + half], dev(p, y, z, k)), ("ax", 0, step), diag)
        for i, p in enumerate(xs):
            put(lambda: (at.at[half], aT.at[k * 2 + half], dev(p, y, z, 1 - k)),
                ("ax", 1, step), beside)
        put(lambda: (at.at[half], aT.at[k * 2 + half], core), ("ax", 1, step), beside)

        @pl.when(diag)
        def _():
            aT[k * 2 + half] = at[half]

        ref = gA.at[k * 2 + half, x]
        for i in (1, 0, 2):
            put(lambda: (ref, ref, dev(xs[i], y, z, k)), ("gg", step, i))
        put(lambda: (ref, ref, core), ("gc", step))

    def part_o(pos):
        return lax.dot_general(aT[pos], w_out[...], TN, preferred_element_type=F32)

    halves = (1 - zh, zh)

    def outputs(c):
        step, half = 1 - c, halves[c]
        held, unheld = k * 2 + half, (1 - k) * 2 + half
        got(lambda: aT.at[held], ("ax", 0, step), no(diag))
        got(lambda: aT.at[unheld], ("ax", 1, step))
        os[c] = part_o(unheld).astype(BF16)
        put(lambda: (os.at[c], orr.at[c], core), ("oc", c))
        o0[c] = part_o(held)
        for i in (0, 2, 1):
            ref = gA.at[held, from_x[i]]
            got(lambda: ref, ("gg", step, i))
            put(lambda: (ref, ref, core), ("gf", step, i))
        got(lambda: orr.at[c], ("oc", c))
        o1[c] = (o0[c] + orr[c].astype(F32)).astype(BF16)
        for i in (1, 0, 2):
            put(lambda: (o1.at[c, :, cols(ys[i])], o1r.at[c, i], dev(x, ys[i], z, k)), ("oy", c, i))
    def features(c):
        step, half = 1 - c, halves[c]
        unheld = (1 - k) * 2 + half
        if c == 0:
            for i in range(3):
                got(lambda: WX.at[from_x[i]], ("wx", i))
        got(lambda: gA.at[unheld, x], ("gc", step))
        for i in (0, 2, 1):
            got(lambda: gA.at[unheld, from_x[i]], ("gf", step, i))
        slab = WX[...].reshape(NX * HIDT, PC)
        for j in range(2):
            g0[c, j] = lax.dot_general(
                gA[j * 2 + half].reshape(NX * HIDT, TOK), slab, TN, preferred_element_type=F32)
        gq[c] = g0[c].astype(BF16)
        for i in (1, 0, 2):
            put(lambda: (gq.at[c, :, rows_at(ys[i] * QR, QR)], g1r.at[c, i],
                         dev(x, ys[i], z, k)), ("gy", c, i))

    zsem = w.block("gz", NL)

    def sums_y(c):
        for i in range(3):
            got(lambda: o1r.at[c, i], ("oy", c, i))
        o2[c] = (
            o1[c, :, cols(y)].astype(F32) + o1r[c, 0].astype(F32)
            + o1r[c, 1].astype(F32) + o1r[c, 2].astype(F32)
        ).astype(BF16)
        for d in range(c, NL):
            target = halves[c] * NL + ls[d]
            put(lambda: (o2.at[c, prow(ls[d])], o2r.at[c, d], dev(x, y, target, k)), ("oz", c, d))

    def feature_sums(c):
        for i in range(3):
            got(lambda: g1r.at[c, i], ("gy", c, i))
        g2[c] = (
            g0[c, :, quarter, :] + g1r[c, 0].astype(F32)
            + g1r[c, 1].astype(F32) + g1r[c, 2].astype(F32)
        ).astype(BF16)
        for j in range(2):
            for e in range(2):
                target = halves[c] * NL + zh * 4 + j * 2 + e
                put(lambda: (g2.at[c, j, pl.ds(e * 16, 16)], g2r.at[zl], dev(x, y, target, k)),
                    zsem(zl), (z != target) if c else None)

    got(lambda: ur.at[1], ("hz", 0))
    activate(1, 1 - zh)
    spread(1, 1 - zh)
    got(lambda: ur.at[0], ("hz", 1))
    activate(0, zh)
    spread(0, zh)
    outputs(0)
    outputs(1)
    features(0)
    features(1)
    sums_y(0)
    sums_y(1)
    feature_sums(0)

    def weight_grad(left, right):
        wide = jnp.concatenate([left((t % 2) * 2 + t // 2) for t in range(4)], axis=1)
        tall = right[...].reshape(4 * TOK, FEAT)
        return jnp.dot(wide, tall, preferred_element_type=F32).astype(BF16)

    g_out[...] = weight_grad(lambda p: aT[p], C)
    stores = [pltpu.make_async_copy(g_out, gout_any, dsem.at[6])]
    stores[0].start()
    feature_sums(1)
    mine_here = zr == zh

    @pl.when(mine_here)
    def _():
        g2r[zl] = g2[1, kt, rows_at(ze * 16, 16), :]

    g_in[...] = weight_grad(lambda p: gA[p, x], N)
    stores.append(pltpu.make_async_copy(g_in, gin_any, dsem.at[7]))
    stores[1].start()

    for n in range(NL):
        got(lambda: g2r.at[n], zsem(n), no(both(mine_here, zl == n)))
    piece = g2r[0].astype(F32)
    for n in range(1, NL):
        piece = piece + g2r[n].astype(F32)
    gp[...] = piece.astype(BF16)
    asem = w.block("gal", NX * 2)
    here = (rows_at(y * QR + ze * 16, 16), cols(x))
    for d in range(NL):
        put(lambda: (gp, gn.at[here], dev(zr * 2 + k, y, zh * NL + ls[d], kt)),
            asem(x * 2 + ze), no(owns) if d == 0 else None)

    @pl.when(owns)
    def _():
        gn[here] = gp[...]

    mine = (prow(zl), cols(y))
    for c in range(2):
        for d in range(c, NL):
            got(lambda: o2r.at[c, d], ("oz", c, d))
    piece = o2[1, prow(zl), :].astype(F32)
    for c in range(2):
        for d in range(c, NL):
            piece = piece + o2r[c, d].astype(F32)
    out[mine] = (x_ref[mine].astype(F32) + piece).astype(BF16)
    lsem = w.block("oal", NL)
    for d in (4, 3, 5, 2, 6, 1, 7):
        put(lambda: (out.at[mine], out.at[mine], dev(x, y, zh * NL + ls[d], k)), lsem(zl))

    mean, rstd = st_ref[:, 0:1], st_ref[:, 1:2]
    sc[...] = (x_ref[...].astype(F32) - mean) * rstd
    stb[...] = jnp.zeros((TOK, TOK), F32)
    group = lax.div(zl, 4)
    groups = (group, 1 - group)

    def strip(n, q):
        return out.at[(rows_at(groups[n] * 64, 64), cols(q))]

    def send_strip(n):
        for i in range(4):
            source = groups[n] * 4 + i
            got(lambda: out.at[prow(source), cols(y)], lsem(source),
                (zl != source) if n == 0 else None)
        for i in (1, 0, 2):
            put(lambda: (strip(n, y), strip(n, y), dev(x, ys[i], z, k)), ("oay", n, i))

    send_strip(0)
    for q in range(NX):
        for e in range(2):
            got(lambda: gn.at[rows_at(y * QR + e * 16, 16), pl.ds(q * PC, PC)], asem(q * 2 + e),
                no(both(owns, x == q, ze == e)))
    for i in (1, 0, 2):
        put(lambda: (gn.at[quarter], gn.at[quarter], dev(x, ys[i], z, k)), ("gay", i))
    gz = gn[quarter, :].astype(F32) * gain
    lane = lax.broadcasted_iota(jnp.int32, (QR, TOK), 1)
    first = jnp.sum(gz, -1, keepdims=True)
    second = jnp.sum(gz * sc[quarter, :], -1, keepdims=True)
    stb[quarter, :] = jnp.where(lane == 0, first, jnp.where(lane == 1, second, 0.0))
    stats[0] = stb[...].T[0:8, :]
    for dx in range(4):
        for dy in range(4):
            if dx or dy:
                put(lambda: (stats.at[0], stats.at[dx * 4 + dy],
                             dev(lax.rem(x + dx, NX), lax.rem(y + dy, NY), z, k)), ("ls", dx, dy))
    send_strip(1)
    for n in range(1, 16):
        got(lambda: stats.at[n], ("ls", n // 4, n % 4))
    sums_all = stats[0]
    for n in range(1, 16):
        sums_all = sums_all + stats[n]
    first, second = unpack_pair(sums_all)
    for i in range(3):
        got(lambda: gn.at[rows_at(from_y[i] * QR, QR)], ("gay", i))
    gz = gn[...].astype(F32) * gain
    delta = rstd * (gz - first / D - sc[...] * (second / D))
    gx[...] = (cot_ref[...].astype(F32) + delta).astype(BF16)
    stores.append(pltpu.make_async_copy(gx, gx_any, dsem.at[9]))
    stores[2].start()
    for n in range(2):
        for i in range(3):
            got(lambda: strip(n, from_y[i]), ("oay", n, i))
    stores.append(pltpu.make_async_copy(out, out_any, dsem.at[8]))
    stores[3].start()
    w.finish()
    for store in stores:
        store.wait()
    assert len(w.sent) <= N_SEND and len(w.slots) <= N_RECV


def hand_kernel(a, b, c, d, ao, bo, co, do, sem):
    copies = [
        pltpu.make_async_copy(src, dst, sem.at[i])
        for i, (src, dst) in enumerate(((a, ao), (b, bo), (c, co), (d, do)))
    ]
    for copy in copies:
        copy.start()
    for copy in copies:
        copy.wait()


def per_device(inputs, cotangent, ln_gain, ln_bias, w_in, w_out):
    dma = pltpu.SemaphoreType.DMA
    tile = jax.ShapeDtypeStruct((TOK, FEAT), BF16)
    grad = jax.ShapeDtypeStruct((HIDT, FEAT), BF16)

    def vb(*shape):
        return pltpu.VMEM(shape, BF16)

    def vf(*shape):
        return pltpu.VMEM(shape, F32)

    results = pl.pallas_call(
        layer_kernel,
        name="layer",
        out_shape=[tile, tile, grad, grad],
        in_specs=[HBM] * 6,
        out_specs=[HBM] * 4,
        scratch_shapes=[
            vb(TOK, FEAT), vb(TOK, FEAT), vf(FEAT), vf(FEAT), vb(HIDT, FEAT), vb(HIDT, FEAT),
            vb(4, TOK, FEAT), vb(4, TOK, FEAT), vb(4, TOK, FEAT), vf(4, 8, TOK), vf(4, 8, TOK),
            vf(2, FEAT), vf(TOK, TOK),
            vf(4, HIDT, TOK), vf(2, HIDT, TOK), vb(2, HIDT, TOK), vb(2, HIDT, TOK),
            vb(3, HIDT, TOK), vb(3, HIDT, TOK), vb(HIDT, TOK), vb(2, HIDT, TOK),
            vb(4, HIDT, TOK), vb(2, HIDT, TOK),
            vb(NX, HIDT, PC), vb(4, NX, HIDT, TOK), vf(2, 2, TOK, PC), vb(2, 2, TOK, PC), vb(2, 3, 2, QR, PC),
            vb(2, 2, QR, PC), vb(NL, PR, PC), vb(PR, PC), vb(TOK, FEAT), vf(TOK, FEAT), vf(TOK, TOK),
            vb(2, TOK, FEAT), vb(2, TOK, FEAT), vf(2, TOK, FEAT), vb(2, TOK, FEAT),
            vb(2, 3, TOK, PC), vb(2, TOK, PC), vb(2, NL, PR, PC), vf(16, 8, TOK),
            vb(TOK, FEAT), vb(TOK, FEAT), vb(HIDT, FEAT), vb(HIDT, FEAT),
            dma((N_SEND,)), dma((N_RECV,)), dma((10,)),
        ],
        compiler_params=pltpu.CompilerParams(
            collective_id=0, has_side_effects=True, vmem_limit_bytes=63 << 20
        ),
    )(inputs, cotangent, ln_gain, ln_bias, w_in.T, w_out)
    out, gx, g_in, g_out = pl.pallas_call(
        hand_kernel,
        name="hand",
        out_shape=[tile, tile, grad, grad],
        in_specs=[VMEM] * 4,
        out_specs=[HBM] * 4,
        scratch_shapes=[dma((4,))],
    )(*results)
    return out, gx, g_in.T, g_out


def solution(mesh):
    return jax.shard_map(
        per_device,
        mesh=mesh,
        in_specs=(
            P("row", "col"),
            P("row", "col"),
            P("col"),
            P("col"),
            P("row", ("section", "col")),
            P(("section", "row"), "col"),
        ),
        out_specs=(
            P("row", "col"),
            P("row", "col"),
            P("row", ("section", "col")),
            P(("section", "row"), "col"),
        ),
        check_vma=False,
    )
```
